512 devices in a mesh: tm: 32 (over y_hi, z), space: 16 (over y_lo, x, core).
Axes of the slice: x: 4, y: 8 (y_hi: 4, y_lo: 2; y = y_hi * 2 + y_lo), z: 8, core: 2. Of those that a mesh axis runs over, the one named last changes fastest.
Arguments:
- previous: float32 [64, 3, 512, 512], P('tm', None, 'space'), may hold values from -6 to 6
- right_side: float32 [64, 3, 512, 512], P('tm', None, 'space'), may hold values from -6 to 6
- kappa: float32 [3, 512, 512], P(None, 'space'), may hold values from 0.2 to 2
- drift: float32 [3, 2], replicated, may hold values from -0.4 to 0.4
- reaction: float32 [3, 3], replicated, may hold values from -0.3 to 1.2, as said below
Outputs:
- new_iterate: float32 [64, 3, 512, 512], P('tm', None, 'space')
- residual: float32 [64, 3, 512, 512], P('tm', None, 'space')
The draws below stay inside these ranges and needn't reach their ends.
Inputs may be any that keep to these rules, and one draw needn't show every extreme that they name: `reaction`: off the diagonal in -0.3 to 0.3, on it 0.6 to 1.2.
All inputs are finite; a program needn't handle non-finite values.
Results may differ from the reference program's by a relative error of at most 0.0003.
Values sent between devices are 32-bit elements; how exact they have to be, the bound alone decides.
A program may use at most 64 MiB of HBM per device.

```python
import math
import jax
import jax.numpy as jnp
from jax import lax

FIELDS = 3
STEPS = 64
SWEEPS = 6
NY = 512
NX = 512


def draw_reaction(key, part):
    key = jax.random.fold_in(key, 11)
    first, second = jax.random.split(key)
    offdiag = jax.random.uniform(first, (FIELDS, FIELDS), jnp.float32, -0.3, 0.3)
    diagonal = jax.random.uniform(second, (FIELDS,), jnp.float32, 0.6, 1.2)
    identity = jnp.eye(FIELDS, dtype=jnp.float32)
    return offdiag * (1.0 - identity) + identity * diagonal[None, :]


def level_of(stream_key, extent, cuts, least, largest):
    def one(axis_at, blocks):
        draws = jax.random.uniform(jax.random.fold_in(jax.random.fold_in(stream_key, 6), axis_at), (blocks,), jnp.float32, least / len(cuts), largest / len(cuts))
        return jnp.repeat(jnp.exp(draws), extent[axis_at] // blocks).reshape((-1,) + (1,) * (len(extent) - axis_at - 1))

    loudness = one(*cuts[0])
    for cut in cuts[1:]:
        loudness = loudness * one(*cut)
    return loudness


def normal_values(stream_key, shape, width, limit, cuts=(), held_as=jnp.bfloat16):
    factor_of = level_of(stream_key, shape, cuts, -0.22, 0.18) if cuts else 1.0
    entries = jax.random.normal(stream_key, shape, jnp.float32) * width * factor_of
    return jnp.minimum(jnp.maximum(entries, -limit), limit).astype(held_as)


def setup_inputs(seed: int = 0) -> dict:
    arg_keys = jax.random.split(jax.random.key(seed), 6)
    previous = normal_values(arg_keys[0], (STEPS, FIELDS, NX, NY), 1.0, 6.0, ((0, 32), (2, 16)), jnp.float32)
    right_side = normal_values(arg_keys[1], (STEPS, FIELDS, NX, NY), 1.0, 6.0, ((0, 32), (2, 16)), jnp.float32)
    kappa = jnp.clip(jnp.exp(math.log(2.0) - 2.3025851 * jax.random.uniform(arg_keys[2], (FIELDS, NX, NY), jnp.float32) ** level_of(arg_keys[2], (FIELDS, NX, NY), ((1, 16),), -0.2, 0.2)), 0.2, 2.0)
    drift = jnp.clip(jax.random.uniform(arg_keys[3], (FIELDS, 2), jnp.float32, -0.4, 0.4), -0.4, 0.4)
    reaction = draw_reaction(jax.random.fold_in(arg_keys[5], 71), 0)
    return {"previous": previous, "right_side": right_side, "kappa": kappa, "drift": drift, "reaction": reaction}


ALPHA = 0.2
highest = lax.Precision.HIGHEST


def time_tables():
    counts = jnp.arange(STEPS, dtype=jnp.int32)
    product = (counts[:, None] * counts[None, :]) % STEPS
    angles = product.astype(jnp.float32) * (2.0 * math.pi / STEPS)
    weights = jnp.power(ALPHA, counts.astype(jnp.float32) / STEPS)
    forward_cos = jnp.cos(angles) * weights[None, :] / STEPS
    forward_sin = jnp.sin(angles) * weights[None, :] / STEPS
    inverse_cos = jnp.cos(angles) / weights[:, None]
    inverse_sin = jnp.sin(angles) / weights[:, None]
    rooted = ALPHA ** (1.0 / STEPS)
    phases = counts.astype(jnp.float32) * (2.0 * math.pi / STEPS)
    eigen_re = 1.0 - rooted * jnp.cos(phases)
    eigen_im = -rooted * jnp.sin(phases)
    return forward_cos, forward_sin, inverse_cos, inverse_sin, eigen_re, eigen_im


def neighbour_terms(center, upper, lower, kappa, drift, react_off):
    plus_y = jnp.roll(center, -1, -1)
    minus_y = jnp.roll(center, 1, -1)
    drift_x = drift[:, 0][:, None, None]
    drift_y = drift[:, 1][:, None, None]
    mixing = jnp.einsum("cd,...dxy->...cxy", react_off, center, precision=highest)
    return (0.5 * drift_x * (upper - lower) + 0.5 * drift_y * (plus_y - minus_y)
            - kappa * (upper + lower + plus_y + minus_y) + mixing)


def reference(previous, right_side, kappa, drift, reaction):
    forward_cos, forward_sin, inverse_cos, inverse_sin, eigen_re, eigen_im = time_tables()
    identity = jnp.eye(FIELDS, dtype=jnp.float32)
    react_off = reaction * (1.0 - identity)
    react_diag = jnp.diagonal(reaction)[:, None, None]
    adjusted = right_side.at[0].add(-ALPHA * previous[STEPS - 1])
    flat = adjusted.reshape(STEPS, -1)
    spectrum_re = jnp.dot(forward_cos, flat, precision=highest).reshape(adjusted.shape)
    spectrum_im = jnp.dot(forward_sin, flat, precision=highest).reshape(adjusted.shape)

    def solve(item):
        hat_re, hat_im, lam_re, lam_im = item
        diag_re = lam_re + (4.0 * kappa + react_diag)
        diag_im = lam_im + jnp.zeros_like(kappa)
        magnitude = diag_re * diag_re + diag_im * diag_im
        inv_re = diag_re / magnitude
        inv_im = -diag_im / magnitude
        sol_re = hat_re * inv_re - hat_im * inv_im
        sol_im = hat_re * inv_im + hat_im * inv_re
        for repeat in range(SWEEPS - 1):
            stacked = jnp.stack([sol_re, sol_im])
            padded = jnp.pad(stacked, ((0, 0), (0, 0), (1, 1), (0, 0)))
            off = neighbour_terms(stacked, padded[:, :, 2:, :], padded[:, :, :-2, :], kappa, drift, react_off)
            resid_re = hat_re - off[0]
            resid_im = hat_im - off[1]
            sol_re, sol_im = resid_re * inv_re - resid_im * inv_im, resid_re * inv_im + resid_im * inv_re
        return sol_re, sol_im

    solved_re, solved_im = lax.map(solve, (spectrum_re, spectrum_im, eigen_re, eigen_im))
    new_iterate = (jnp.dot(inverse_cos, solved_re.reshape(STEPS, -1), precision=highest)
                   + jnp.dot(inverse_sin, solved_im.reshape(STEPS, -1), precision=highest)).reshape(adjusted.shape)
    padded = jnp.pad(new_iterate, ((0, 0), (0, 0), (1, 1), (0, 0)))
    operated = (4.0 * kappa + react_diag) * new_iterate + neighbour_terms(
        new_iterate, padded[:, :, 2:, :], padded[:, :, :-2, :], kappa, drift, react_off)
    earlier = jnp.concatenate([jnp.zeros_like(new_iterate[:1]), new_iterate[:-1]], 0)
    residual = right_side - (new_iterate + operated - earlier)
    return new_iterate, residual
```

```python
import functools

import jax
import jax.numpy as jnp
from jax import lax
from jax.experimental import pallas as pl
from jax.experimental.pallas import tpu as pltpu
from jax.sharding import PartitionSpec as P

ALPHA = 0.2
TM = 32
MESH = pl.DeviceIdType.MESH
F32 = jnp.float32


def place_of(tile, space):
    r, c = tile // 8, tile % 8
    odd = space % 2
    q = r + odd * (3 - 2 * r)
    half = c // 4
    y = (c % 4) + half * (3 - 2 * (c % 4))
    z = q + half * (7 - 2 * q)
    return y * 8 + z


def tile_of(tm, space):
    y, z = tm // 8, tm % 8
    half = z // 4
    q = z + half * (7 - 2 * z)
    c = half * 4 + y + half * (3 - 2 * y)
    odd = space % 2
    r = q + odd * (3 - 2 * q)
    return r * 8 + c


def kernel(
    b_hbm, prev_hbm, kappa_hbm, drift_s, react_s,
    out_u, out_res,
    bv, prev_v, kap, pack, held, prev_r, u5, u6, back5, back6, wn,
    row_s, row_r, col_s, col_r, edge_s, edge_r, coef,
    in_sem, a_send, a_recv, p_send, p_recv, h_send, h_recv, r5_send, r5_recv, r6_send, r6_recv, e_send, e_recv,
):
    me = lax.axis_index("tm")
    sp = lax.axis_index("space")
    spaces = lax.axis_size("space")
    tile = tile_of(me, sp)
    r, c = tile // 8, tile % 8

    load_b = pltpu.make_async_copy(b_hbm, bv, in_sem.at[0])
    load_k = pltpu.make_async_copy(kappa_hbm, kap, in_sem.at[1])
    load_p = pltpu.make_async_copy(prev_hbm.at[1], prev_v, in_sem.at[2])
    load_b.start()
    load_k.start()
    last = me == TM - 1

    @pl.when(last)
    def _():
        load_p.start()

    row_r[...] = jnp.zeros_like(row_r)
    edge_r[...] = jnp.zeros_like(edge_r)

    barrier = pltpu.get_barrier_semaphore()

    @pl.loop(1, TM)
    def _(o):
        pl.semaphore_signal(barrier, inc=1, device_id=((me + o) % TM, sp), device_id_type=MESH)

    @pl.when(sp > 0)
    def _():
        pl.semaphore_signal(barrier, inc=1, device_id=(me, sp - 1), device_id_type=MESH)

    @pl.when(sp < spaces - 1)
    def _():
        pl.semaphore_signal(barrier, inc=1, device_id=(me, sp + 1), device_id_type=MESH)

    lane = lax.broadcasted_iota(jnp.int32, (8, 128), 1)
    sub = lax.broadcasted_iota(jnp.int32, (8, 128), 0)
    odd = lane >= 64
    inner = lane % 64

    load_b.wait()

    @pl.loop(0, 16)
    def _(i):
        rr, cp = i // 4, i % 4
        rows = pl.ds(pl.multiple_of(rr * 8, 8), 8)
        cols = pl.ds(pl.multiple_of(cp * 128, 128), 128)
        for f in range(3):
            first = bv[0, f, rows, cols]
            second = bv[1, f, rows, cols]
            pack[rr * 8 + cp * 2, f] = jnp.where(odd, pltpu.roll(second, 64, 1), first)
            pack[rr * 8 + cp * 2 + 1, f] = jnp.where(odd, second, pltpu.roll(first, 64, 1))

    pl.semaphore_wait(barrier, TM - 1 + jnp.where(sp > 0, 1, 0) + jnp.where(sp < spaces - 1, 1, 0))

    def send_forward(o):
        p = (me + o) % TM
        return pltpu.make_async_remote_copy(
            src_ref=pack.at[tile_of(p, sp)], dst_ref=held.at[me], send_sem=a_send, recv_sem=a_recv,
            device_id=(p, sp), device_id_type=MESH)

    @pl.loop(1, TM)
    def _(o):
        send_forward(o).start()

    own = pltpu.make_async_copy(pack.at[tile], held.at[me], in_sem.at[3])
    own.start()

    def prev_part(t):
        rows = pl.ds(pl.multiple_of((t // 8) * 8, 8), 8)
        cols = pl.ds(pl.multiple_of(((t % 8) // 2) * 128, 128), 128)
        return prev_v.at[:, rows, cols]

    @pl.when(last)
    def _():
        load_p.wait()

        @pl.loop(0, TM - 1)
        def _(p):
            pltpu.make_async_remote_copy(
                src_ref=prev_part(tile_of(p, sp)), dst_ref=prev_r, send_sem=p_send, recv_sem=p_recv,
                device_id=(p, sp), device_id_type=MESH).start()

        mine = pltpu.make_async_copy(prev_part(tile), prev_r, in_sem.at[2])
        mine.start()
        mine.wait()

    load_k.wait()
    rows = pl.ds(pl.multiple_of(r * 8, 8), 8)
    cols = pl.ds(pl.multiple_of((c // 2) * 128, 128), 128)
    upper_half = (c % 2) == 1
    keep = jnp.where(upper_half, lane, 127 - lane) >= 64
    for f in range(3):
        k = kap[f, rows, cols]
        k = jnp.where(keep, k, pltpu.roll(k, 64, 1))
        g = 1.0 / (1.0 + 4.0 * k + react_s[f, f])
        g2 = g * g
        g4 = g2 * g2
        g8 = g4 * g4
        g16 = g8 * g8
        g32 = g16 * g16
        g64 = g32 * g32
        coef[0, f] = 0.5 * drift_s[f, 0] - k
        coef[1, f] = -0.5 * drift_s[f, 0] - k
        coef[2, f] = 0.5 * drift_s[f, 1] - k
        coef[3, f] = -0.5 * drift_s[f, 1] - k
        coef[4, f] = g
        coef[5, f] = ALPHA / (1.0 - ALPHA * g64)

    own.wait()
    pltpu.make_async_copy(pack.at[pl.ds(0, TM - 1)], held.at[pl.ds(0, TM - 1)], a_recv).wait()

    @pl.when(jnp.logical_not(last))
    def _():
        pltpu.make_async_copy(prev_r, prev_r, p_recv).wait()

    for f in range(3):
        p = prev_r[f]
        p = jnp.where(keep, p, pltpu.roll(p, 64, 1))
        held[0, f] = held[0, f] - ALPHA * jnp.where(odd, 0.0, p)

    zero = jnp.zeros((8, 128), F32)

    left = place_of(r * 8 + (c + 7) % 8, sp)
    right = place_of(r * 8 + (c + 1) % 8, sp)
    up_in = r > 0
    dn_in = r < 3
    has_up = jnp.logical_or(up_in, sp > 0)
    has_dn = jnp.logical_or(dn_in, sp < spaces - 1)
    up_tm = jnp.where(up_in, place_of(jnp.maximum(r - 1, 0) * 8 + c, sp), me)
    up_sp = jnp.where(up_in, sp, jnp.maximum(sp - 1, 0))
    dn_tm = jnp.where(dn_in, place_of(jnp.minimum(r + 1, 3) * 8 + c, sp), me)
    dn_sp = jnp.where(dn_in, sp, jnp.minimum(sp + 1, spaces - 1))

    def row_copy(j, way):
        return pltpu.make_async_remote_copy(
            src_ref=row_s.at[j, way], dst_ref=row_r.at[j, way], send_sem=h_send.at[j, way], recv_sem=h_recv.at[j, way],
            device_id=((up_tm, up_sp), (dn_tm, dn_sp))[way], device_id_type=MESH)

    def col_copy(j, way):
        return pltpu.make_async_remote_copy(
            src_ref=col_s.at[j, way], dst_ref=col_r.at[j, way], send_sem=h_send.at[j, 2 + way],
            recv_sem=h_recv.at[j, 2 + way], device_id=((left, right)[way], sp), device_id_type=MESH)

    def sweep(j, src, dst):
        def step(m, carry):
            out = []
            v = [src[m, f] for f in range(3)] if src is not None else None
            for f in range(3):
                g = coef[4, f]
                rest = held[m, f]
                if src is not None:
                    below = jnp.where(sub == 7, row_r[j, 0, f, pl.ds(m, 1), :], pltpu.roll(v[f], 7, 0))
                    above = jnp.where(sub == 0, row_r[j, 1, f, pl.ds(m, 1), :], pltpu.roll(v[f], 1, 0))
                    after = jnp.where(inner == 63, pltpu.roll(col_r[j, 0, f], 63 - m, 1), pltpu.roll(v[f], 127, 1))
                    before = jnp.where(inner == 0, pltpu.roll(col_r[j, 1, f], (128 - m) % 128, 1), pltpu.roll(v[f], 1, 1))
                    d, e = [i for i in range(3) if i != f]
                    off = (coef[0, f] * below + coef[1, f] * above + coef[2, f] * after + coef[3, f] * before
                           + (react_s[f, d] * v[d] + react_s[f, e] * v[e]))
                    rest = rest - off
                x = g * rest
                swapped = pltpu.roll(x, 64, 1)
                both = jnp.where(odd, x, swapped) + g * jnp.where(odd, swapped, x)
                total = both + (g * g) * carry[f]
                dst[m, f] = jnp.where(odd, total, x + g * carry[f])
                out.append(total)
            return tuple(out)

        ends = lax.fori_loop(0, TM, step, (zero, zero, zero))
        return tuple(coef[5, f] * ends[f] for f in range(3))

    def correct(j, dst, wrap, halo):
        def step(m, carry):
            out = []
            for f in range(3):
                g = coef[4, f]
                g2 = g * g
                w, lft, rgt = carry[3 * f:3 * f + 3]
                u = dst[m, f] + jnp.where(odd, g2, g) * w
                dst[m, f] = u
                w = g2 * w
                if halo:
                    row_s[j, 0, f, pl.ds(m, 1), :] = u[0:1]
                    row_s[j, 1, f, pl.ds(m, 1), :] = u[7:8]
                    here = inner == m
                    lft = jnp.where(here, pltpu.roll(u, m, 1), lft)
                    rgt = jnp.where(here, pltpu.roll(u, m + 65, 1), rgt)
                out += [w, lft, rgt]
            return tuple(out)

        start = []
        for f in range(3):
            start += [wrap[f], zero, zero]
        ends = lax.fori_loop(0, TM, step, tuple(start))
        if not halo:
            return
        for f in range(3):
            col_s[j, 0, f] = ends[3 * f + 1]
            col_s[j, 1, f] = ends[3 * f + 2]

        @pl.when(has_up)
        def _():
            row_copy(j, 0).start()

        @pl.when(has_dn)
        def _():
            row_copy(j, 1).start()

        col_copy(j, 0).start()
        col_copy(j, 1).start()

    def await_halo(j):
        @pl.when(has_dn)
        def _():
            row_copy(j, 0).wait_recv()

        @pl.when(has_up)
        def _():
            row_copy(j, 1).wait_recv()

        col_copy(j, 0).wait_recv()
        col_copy(j, 1).wait_recv()

    correct(0, u5, sweep(0, None, u5), True)

    @pl.loop(0, 4)
    def _(j):
        await_halo(j)
        correct(j + 1, u5, sweep(j, u5, u5), True)

    def send_back(o, src, dst, send_sem, recv_sem):
        p = (me + o) % TM
        return pltpu.make_async_remote_copy(
            src_ref=src.at[p], dst_ref=dst.at[tile], send_sem=send_sem, recv_sem=recv_sem,
            device_id=(p, sp), device_id_type=MESH)

    @pl.loop(1, TM)
    def _(o):
        send_back(o, u5, back5, r5_send, r5_recv).start()

    own5 = pltpu.make_async_copy(u5.at[me], back5.at[tile], in_sem.at[0])
    own5.start()

    await_halo(4)
    correct(4, u6, sweep(4, u5, u6), False)

    @pl.loop(1, TM)
    def _(o):
        send_back(o, u6, back6, r6_send, r6_recv).start()

    own6 = pltpu.make_async_copy(u6.at[me], back6.at[tile], in_sem.at[1])
    own6.start()

    own5.wait()
    own6.wait()
    some = pl.ds(0, TM - 1)
    pltpu.make_async_copy(u5.at[some], back5.at[some], r5_recv).wait()
    pltpu.make_async_copy(u6.at[some], back6.at[some], r6_recv).wait()

    first_step = jnp.where(me == 0, 1.0, 0.0)

    @pl.loop(0, 16)
    def _(i):
        rr, cp = i // 4, i % 4
        rows = pl.ds(pl.multiple_of(rr * 8, 8), 8)
        cols = pl.ds(pl.multiple_of(cp * 128, 128), 128)
        t = rr * 8 + cp * 2
        for f in range(3):
            a6, b6 = back6[t, f], back6[t + 1, f]
            a5, b5 = back5[t, f], back5[t + 1, f]
            n0 = jnp.where(odd, pltpu.roll(b6, 64, 1), a6)
            n1 = jnp.where(odd, b6, pltpu.roll(a6, 64, 1))
            o0 = jnp.where(odd, pltpu.roll(b5, 64, 1), a5)
            o1 = jnp.where(odd, b5, pltpu.roll(a5, 64, 1))
            out_u[0, f, rows, cols] = n0
            out_u[1, f, rows, cols] = n1
            wn[0, f, rows, cols] = o0 * (1.0 - first_step) - n0
            wn[1, f, rows, cols] = o1 - n1

    for s in range(2):
        for f in range(3):
            i = s * 3 + f
            edge_s[0, i:i + 1, :] = wn[s, f, 0:1, :]
            edge_s[1, i:i + 1, :] = wn[s, f, 31:32, :]

    def edge_copy(way):
        return pltpu.make_async_remote_copy(
            src_ref=edge_s.at[way], dst_ref=edge_r.at[way], send_sem=e_send.at[way], recv_sem=e_recv.at[way],
            device_id=(me, (jnp.maximum(sp - 1, 0), jnp.minimum(sp + 1, spaces - 1))[way]), device_id_type=MESH)

    @pl.when(sp > 0)
    def _():
        edge_copy(0).start()

    @pl.when(sp < spaces - 1)
    def _():
        edge_copy(1).start()

    @pl.when(sp < spaces - 1)
    def _():
        edge_copy(0).wait_recv()

    @pl.when(sp > 0)
    def _():
        edge_copy(1).wait_recv()

    tall = lax.broadcasted_iota(jnp.int32, (32, 512), 0)
    for s in range(2):
        w = [wn[s, f] for f in range(3)]
        for f in range(3):
            i = s * 3 + f
            k = kap[f]
            below = jnp.where(tall == 31, edge_r[0, i:i + 1, :], pltpu.roll(w[f], 31, 0))
            above = jnp.where(tall == 0, edge_r[1, i:i + 1, :], pltpu.roll(w[f], 1, 0))
            after = pltpu.roll(w[f], 511, 1)
            before = pltpu.roll(w[f], 1, 1)
            d, e = [n for n in range(3) if n != f]
            res = (0.5 * drift_s[f, 0] * (below - above) + 0.5 * drift_s[f, 1] * (after - before)
                   - k * (below + above + after + before) + (react_s[f, d] * w[d] + react_s[f, e] * w[e]))
            if s == 0:
                res = res + first_step * (bv[0, f] - (1.0 + 4.0 * k + react_s[f, f]) * out_u[0, f])
            out_res[s, f] = res

    pltpu.make_async_copy(pack.at[some], held.at[some], a_send).wait()
    pltpu.make_async_copy(u5.at[some], back5.at[some], r5_send).wait()
    pltpu.make_async_copy(u6.at[some], back6.at[some], r6_send).wait()

    @pl.when(last)
    def _():
        pltpu.make_async_copy(pack.at[some], held.at[some], p_send).wait()

    @pl.loop(0, 5)
    def _(j):
        @pl.when(has_up)
        def _():
            row_copy(j, 0).wait_send()

        @pl.when(has_dn)
        def _():
            row_copy(j, 1).wait_send()

        col_copy(j, 0).wait_send()
        col_copy(j, 1).wait_send()

    @pl.when(sp > 0)
    def _():
        edge_copy(0).wait_send()

    @pl.when(sp < spaces - 1)
    def _():
        edge_copy(1).wait_send()


def shards(previous, right_side, kappa, drift, reaction):
    anyspace = pl.BlockSpec(memory_space=pl.ANY)
    smem = pl.BlockSpec(memory_space=pltpu.SMEM)
    vmem = pl.BlockSpec(memory_space=pltpu.VMEM)
    shape = jax.ShapeDtypeStruct(right_side.shape, F32)
    dma = pltpu.SemaphoreType.DMA
    held = pltpu.VMEM((TM, 3, 8, 128), F32)
    return pl.pallas_call(
        kernel,
        out_shape=(shape, shape),
        in_specs=[anyspace, anyspace, anyspace, smem, smem],
        out_specs=(vmem, vmem),
        scratch_shapes=[
            pltpu.VMEM((2, 3, 32, 512), F32),
            pltpu.VMEM((3, 32, 512), F32),
            pltpu.VMEM((3, 32, 512), F32),
            held, held,
            pltpu.VMEM((3, 8, 128), F32),
            held, held, held, held,
            pltpu.VMEM((2, 3, 32, 512), F32),
            pltpu.VMEM((5, 2, 3, 32, 128), F32),
            pltpu.VMEM((5, 2, 3, 32, 128), F32),
            pltpu.VMEM((5, 2, 3, 8, 128), F32),
            pltpu.VMEM((5, 2, 3, 8, 128), F32),
            pltpu.VMEM((2, 8, 512), F32),
            pltpu.VMEM((2, 8, 512), F32),
            pltpu.VMEM((6, 3, 8, 128), F32),
            dma((4,)),
            dma, dma, dma, dma,
            dma((5, 4)), dma((5, 4)),
            dma, dma, dma, dma,
            dma((2,)), dma((2,)),
        ],
        compiler_params=pltpu.CompilerParams(
            collective_id=0, has_side_effects=True, vmem_limit_bytes=40 * 1024 * 1024),
    )(right_side, previous, kappa, drift, reaction)


def solution(mesh):
    in_specs = (
        P("tm", None, "space", None),
        P("tm", None, "space", None),
        P(None, "space", None),
        P(),
        P(),
    )
    out_specs = (P("tm", None, "space", None), P("tm", None, "space", None))
    return jax.shard_map(shards, mesh=mesh, in_specs=in_specs, out_specs=out_specs, check_vma=False)
```

```python
import functools

import jax
import jax.numpy as jnp
from jax import lax
from jax.experimental import pallas as pl
from jax.experimental.pallas import tpu as pltpu
from jax.sharding import PartitionSpec as P

ALPHA = 0.2
TM = 32
MESH = pl.DeviceIdType.MESH
F32 = jnp.float32


def place_of(tile, space):
    r, c = tile // 8, tile % 8
    odd = space % 2
    q = r + odd * (3 - 2 * r)
    half = c // 4
    y = (c % 4) + half * (3 - 2 * (c % 4))
    z = q + half * (7 - 2 * q)
    return y * 8 + z


def tile_of(tm, space):
    y, z = tm // 8, tm % 8
    half = z // 4
    q = z + half * (7 - 2 * z)
    c = half * 4 + y + half * (3 - 2 * y)
    odd = space % 2
    r = q + odd * (3 - 2 * q)
    return r * 8 + c


HOPS = [(dy, dz) for dz in (4, 3, 5, 2, 6, 1, 7, 0) for dy in (2, 1, 3, 0) if (dy, dz) != (0, 0)]
UNROLL = 8


def kernel(
    b_hbm, prev_hbm, kappa_hbm, drift_s, react_s,
    out_u, out_res,
    bv, prev_v, kap, pack, msgs, held, prev_r, ua, ub, m5, m6, back5, back6, wn,
    row_s, row_r, col_s, col_r, edge_s, edge_r, coef, row_g, col_g,
    in_sem, a_send, a_recv, p_send, p_recv, h_send, h_recv, r5_send, r5_recv, r6_send, r6_recv, e_send, e_recv,
):
    me = lax.axis_index("tm")
    sp = lax.axis_index("space")
    spaces = lax.axis_size("space")
    tile = tile_of(me, sp)
    r, c = tile // 8, tile % 8
    my, mz = me // 8, me % 8
    peers = [((my + dy) % 4) * 8 + (mz + dz) % 8 for dy, dz in HOPS]

    load_b = pltpu.make_async_copy(b_hbm, bv, in_sem.at[0])
    load_k = pltpu.make_async_copy(kappa_hbm, kap, in_sem.at[1])
    load_p = pltpu.make_async_copy(prev_hbm.at[1], prev_v, in_sem.at[2])
    load_b.start()
    load_k.start()
    last = me == TM - 1

    @pl.when(last)
    def _():
        load_p.start()

    row_r[...] = jnp.zeros_like(row_r)
    edge_r[...] = jnp.zeros_like(edge_r)

    barrier = pltpu.get_barrier_semaphore()
    for p in peers:
        pl.semaphore_signal(barrier, inc=1, device_id=(p, sp), device_id_type=MESH)

    @pl.when(sp > 0)
    def _():
        pl.semaphore_signal(barrier, inc=1, device_id=(me, sp - 1), device_id_type=MESH)

    @pl.when(sp < spaces - 1)
    def _():
        pl.semaphore_signal(barrier, inc=1, device_id=(me, sp + 1), device_id_type=MESH)

    lane = lax.broadcasted_iota(jnp.int32, (8, 128), 1)
    sub = lax.broadcasted_iota(jnp.int32, (8, 128), 0)
    high = lane >= 64
    inner = lane % 64
    zero = jnp.zeros((8, 128), F32)

    def swap(x):
        return pltpu.roll(x, 64, 1)

    load_b.wait()

    @pl.loop(0, 4)
    def _(rr):
        rows = pl.ds(pl.multiple_of(rr * 8, 8), 8)
        for cp in range(4):
            cols = pl.ds(cp * 128, 128)
            for f in range(3):
                first = bv[0, f, rows, cols]
                second = bv[1, f, rows, cols]
                pack[rr * 8 + cp * 2, f] = jnp.where(high, swap(second), first)
                pack[rr * 8 + cp * 2 + 1, f] = jnp.where(high, second, swap(first))

    pl.semaphore_wait(barrier, TM - 1 + jnp.where(sp > 0, 1, 0) + jnp.where(sp < spaces - 1, 1, 0))

    def prev_part(t):
        rows = pl.ds(pl.multiple_of((t // 8) * 8, 8), 8)
        cols = pl.ds(pl.multiple_of(((t % 8) // 2) * 128, 128), 128)
        return prev_v.at[:, rows, cols]

    @pl.when(last)
    def _():
        load_p.wait()

        @pl.loop(0, TM - 1)
        def _(p):
            pltpu.make_async_remote_copy(
                src_ref=prev_part(tile_of(p, sp)), dst_ref=prev_r, send_sem=p_send, recv_sem=p_recv,
                device_id=(p, sp), device_id_type=MESH).start()

        mine = pltpu.make_async_copy(prev_part(tile), prev_r, in_sem.at[2])
        mine.start()
        mine.wait()

    for p in peers:
        pltpu.make_async_remote_copy(
            src_ref=pack.at[tile_of(p, sp)], dst_ref=msgs.at[me], send_sem=a_send, recv_sem=a_recv,
            device_id=(p, sp), device_id_type=MESH).start()
    own = pltpu.make_async_copy(pack.at[tile], msgs.at[me], in_sem.at[3])
    own.start()

    load_k.wait()
    rows = pl.ds(pl.multiple_of(r * 8, 8), 8)
    cols = pl.ds(pl.multiple_of((c // 2) * 128, 128), 128)
    upper_half = (c % 2) == 1
    keep = jnp.where(upper_half, lane, 127 - lane) >= 64
    ratio = []
    for f in range(3):
        k = kap[f, rows, cols]
        k = jnp.where(keep, k, swap(k))
        g = 1.0 / (1.0 + 4.0 * k + react_s[f, f])
        ratio.append(g)
        g2 = g * g
        g4 = g2 * g2
        g8 = g4 * g4
        g16 = g8 * g8
        g32 = g16 * g16
        below = g * (0.5 * drift_s[0, f] - k)
        above = g * (-0.5 * drift_s[0, f] - k)
        after = g * (0.5 * drift_s[1, f] - k)
        before = g * (-0.5 * drift_s[1, f] - k)
        d, e = [n for n in range(3) if n != f]
        coef[0, f] = jnp.where(sub == 7, 0.0, below)
        coef[1, f] = jnp.where(sub == 0, 0.0, above)
        coef[2, f] = jnp.where(inner == 63, 0.0, after)
        coef[3, f] = jnp.where(inner == 0, 0.0, before)
        coef[4, f] = g * react_s[f, d]
        coef[5, f] = g * react_s[f, e]
        coef[6, f] = jnp.where(sub == 7, below, jnp.where(sub == 0, above, 0.0))
        coef[7, f] = jnp.where(inner == 63, after, jnp.where(inner == 0, before, 0.0))
        coef[8, f] = g
        coef[9, f] = g32
        coef[10, f] = 1.0 / (1.0 - ALPHA * (g32 * g32))

    def power(i, carry):
        carry = list(carry)
        for u in range(UNROLL):
            m = i * UNROLL + u
            here = inner == m
            for f in range(3):
                w, lft, rgt = carry[3 * f:3 * f + 3]
                row_g[0, f, pl.ds(m, 1), :] = w[0:1]
                row_g[1, f, pl.ds(m, 1), :] = w[7:8]
                lft = jnp.where(here, pltpu.roll(w, m, 1), lft)
                rgt = jnp.where(here, pltpu.roll(w, m + 65, 1), rgt)
                carry[3 * f:3 * f + 3] = [w * coef[8, f], lft, rgt]
        return tuple(carry)

    start = []
    for f in range(3):
        start += [ratio[f], zero, zero]
    ends = lax.fori_loop(0, 32 // UNROLL, power, tuple(start))
    for f in range(3):
        col_g[0, f] = ends[3 * f + 1]
        col_g[1, f] = ends[3 * f + 2]

    left = place_of(r * 8 + (c + 7) % 8, sp)
    right = place_of(r * 8 + (c + 1) % 8, sp)
    up_in = r > 0
    dn_in = r < 3
    has_up = jnp.logical_or(up_in, sp > 0)
    has_dn = jnp.logical_or(dn_in, sp < spaces - 1)
    up_tm = jnp.where(up_in, place_of(jnp.maximum(r - 1, 0) * 8 + c, sp), me)
    up_sp = jnp.where(up_in, sp, jnp.maximum(sp - 1, 0))
    dn_tm = jnp.where(dn_in, place_of(jnp.minimum(r + 1, 3) * 8 + c, sp), me)
    dn_sp = jnp.where(dn_in, sp, jnp.minimum(sp + 1, spaces - 1))

    def row_copy(j, way):
        return pltpu.make_async_remote_copy(
            src_ref=row_s.at[j, way], dst_ref=row_r.at[j, way], send_sem=h_send.at[j, way], recv_sem=h_recv.at[j, way],
            device_id=((up_tm, up_sp), (dn_tm, dn_sp))[way], device_id_type=MESH)

    def col_copy(j, way):
        return pltpu.make_async_remote_copy(
            src_ref=col_s.at[j, way], dst_ref=col_r.at[j, way], send_sem=h_send.at[j, 2 + way],
            recv_sem=h_recv.at[j, 2 + way], device_id=((left, right)[way], sp), device_id_type=MESH)

    def carry_in(ends):
        out = []
        for f in range(3):
            end, other = ends[f], swap(ends[f])
            g32 = coef[9, f]
            final = (jnp.where(high, end, other) + g32 * jnp.where(high, other, end)) * coef[10, f]
            wrap = ALPHA * final
            out.append(jnp.where(high, other + g32 * wrap, wrap))
        return out

    def send_halo(j, came, lefts, rights):
        for f in range(3):
            row_s[j, 0, f] = row_s[j, 0, f] + row_g[0, f] * came[f][0:1]
            row_s[j, 1, f] = row_s[j, 1, f] + row_g[1, f] * came[f][7:8]
            col_s[j, 0, f] = lefts[f] + col_g[0, f] * jnp.where(high, came[f][:, 64:65], came[f][:, 0:1])
            col_s[j, 1, f] = rights[f] + col_g[1, f] * jnp.where(high, came[f][:, 127:128], came[f][:, 63:64])

        @pl.when(has_up)
        def _():
            row_copy(j, 0).start()

        @pl.when(has_dn)
        def _():
            row_copy(j, 1).start()

        col_copy(j, 0).start()
        col_copy(j, 1).start()

    def await_halo(j):
        @pl.when(has_dn)
        def _():
            row_copy(j, 0).wait_recv()

        @pl.when(has_up)
        def _():
            row_copy(j, 1).wait_recv()

        col_copy(j, 0).wait_recv()
        col_copy(j, 1).wait_recv()

    def pack_border(j, m, f, u, lft, rgt):
        here = inner == m
        row_s[j, 0, f, pl.ds(m, 1), :] = u[0:1]
        row_s[j, 1, f, pl.ds(m, 1), :] = u[7:8]
        return jnp.where(here, pltpu.roll(u, m, 1), lft), jnp.where(here, pltpu.roll(u, m + 65, 1), rgt)

    def interior(came, src, dst):
        def step(i, carry):
            carry = list(carry)
            for u in range(UNROLL):
                m = i * UNROLL + u
                v = []
                for f in range(3):
                    carry[f] = carry[f] * coef[8, f]
                    v.append(src[m, f] + carry[f])
                    if dst is not src:
                        src[m, f] = v[f]
                for f in range(3):
                    d, e = [n for n in range(3) if n != f]
                    off = (coef[0, f] * pltpu.roll(v[f], 7, 0) + coef[1, f] * pltpu.roll(v[f], 1, 0)
                           + coef[2, f] * pltpu.roll(v[f], 127, 1) + coef[3, f] * pltpu.roll(v[f], 1, 1)
                           + coef[4, f] * v[d] + coef[5, f] * v[e])
                    dst[m, f] = held[m, f] - off
            return tuple(carry)

        lax.fori_loop(0, 32 // UNROLL, step, tuple(came))

    def border_scan(j, dst, halo):
        def step(i, carry):
            carry = list(carry)
            for u in range(UNROLL):
                m = i * UNROLL + u
                for f in range(3):
                    before, lft, rgt = carry[3 * f:3 * f + 3]
                    rows = jnp.where(sub == 0, row_r[j, 1, f, pl.ds(m, 1), :], row_r[j, 0, f, pl.ds(m, 1), :])
                    cols = jnp.where(inner == 0, pltpu.roll(col_r[j, 1, f], (128 - m) % 128, 1),
                                     pltpu.roll(col_r[j, 0, f], 63 - m, 1))
                    x = dst[m, f] - (coef[6, f] * rows + coef[7, f] * cols)
                    now = x + coef[8, f] * before
                    dst[m, f] = now
                    if halo:
                        lft, rgt = pack_border(j + 1, m, f, now, lft, rgt)
                    carry[3 * f:3 * f + 3] = [now, lft, rgt]
            return tuple(carry)

        ends = lax.fori_loop(0, 32 // UNROLL, step, (zero,) * 9)
        return ends[0::3], ends[1::3], ends[2::3]

    own.wait()
    some = pl.ds(0, TM - 1)
    pltpu.make_async_copy(pack.at[some], msgs.at[some], a_recv).wait()

    @pl.when(jnp.logical_not(last))
    def _():
        pltpu.make_async_copy(prev_r, prev_r, p_recv).wait()

    for f in range(3):
        p = prev_r[f]
        p = jnp.where(keep, p, swap(p))
        msgs[0, f] = msgs[0, f] - ALPHA * jnp.where(high, 0.0, p)

    def first(i, carry):
        carry = list(carry)
        for u in range(UNROLL // 2):
            h = i * (UNROLL // 2) + u
            for f in range(3):
                before, lft, rgt = carry[3 * f:3 * f + 3]
                g = coef[8, f]
                a, b = msgs[h, f], msgs[16 + h, f]
                even = g * jnp.where(high, swap(b), a)
                odd = g * jnp.where(high, b, swap(a))
                held[2 * h, f] = even
                held[2 * h + 1, f] = odd
                now = even + g * before
                ua[2 * h, f] = now
                lft, rgt = pack_border(0, 2 * h, f, now, lft, rgt)
                now = odd + g * now
                ua[2 * h + 1, f] = now
                lft, rgt = pack_border(0, 2 * h + 1, f, now, lft, rgt)
                carry[3 * f:3 * f + 3] = [now, lft, rgt]
        return tuple(carry)

    ends = lax.fori_loop(0, 32 // UNROLL, first, (zero,) * 9)
    came = carry_in(ends[0::3])
    send_halo(0, came, ends[1::3], ends[2::3])

    def sweep(j, came):
        interior(came, ua, ua)
        await_halo(j)
        ends, lefts, rights = border_scan(j, ua, True)
        came = carry_in(ends)
        send_halo(j + 1, came, lefts, rights)
        return tuple(came)

    came = lax.fori_loop(0, 4, sweep, tuple(came))

    def to_messages(src, dst, came):
        def step(i, carry):
            carry = list(carry)
            for u in range(UNROLL // 2):
                h = i * (UNROLL // 2) + u
                for f in range(3):
                    even, odd = src[2 * h, f], src[2 * h + 1, f]
                    if came is not None:
                        w = carry[f] * coef[8, f]
                        even = even + w
                        w = w * coef[8, f]
                        odd = odd + w
                        carry[f] = w
                    dst[h, f] = jnp.where(high, swap(odd), even)
                    dst[16 + h, f] = jnp.where(high, odd, swap(even))
            return tuple(carry)

        lax.fori_loop(0, 32 // UNROLL, step, tuple(came) if came is not None else ())

    def send_back(src, dst, send_sem, recv_sem, own_sem):
        for p in peers:
            pltpu.make_async_remote_copy(
                src_ref=src.at[p], dst_ref=dst.at[tile], send_sem=send_sem, recv_sem=recv_sem,
                device_id=(p, sp), device_id_type=MESH).start()
        own = pltpu.make_async_copy(src.at[me], dst.at[tile], own_sem)
        own.start()
        return own

    interior(came, ua, ub)
    to_messages(ua, m5, None)
    own5 = send_back(m5, back5, r5_send, r5_recv, in_sem.at[0])
    await_halo(4)
    ends, _, _ = border_scan(4, ub, False)
    to_messages(ub, m6, carry_in(ends))
    own6 = send_back(m6, back6, r6_send, r6_recv, in_sem.at[1])

    own5.wait()
    own6.wait()
    pltpu.make_async_copy(m5.at[some], back5.at[some], r5_recv).wait()
    pltpu.make_async_copy(m6.at[some], back6.at[some], r6_recv).wait()

    first_step = jnp.where(me == 0, 1.0, 0.0)

    @pl.loop(0, 4)
    def _(rr):
        rows = pl.ds(pl.multiple_of(rr * 8, 8), 8)
        for cp in range(4):
            cols = pl.ds(cp * 128, 128)
            t = rr * 8 + cp * 2
            for f in range(3):
                a6, b6 = back6[t, f], back6[t + 1, f]
                a5, b5 = back5[t, f], back5[t + 1, f]
                n0 = jnp.where(high, swap(b6), a6)
                n1 = jnp.where(high, b6, swap(a6))
                o0 = jnp.where(high, swap(b5), a5)
                o1 = jnp.where(high, b5, swap(a5))
                out_u[0, f, rows, cols] = n0
                out_u[1, f, rows, cols] = n1
                wn[0, f, rows, cols] = o0 * (1.0 - first_step) - n0
                wn[1, f, rows, cols] = o1 - n1

    for s in range(2):
        for f in range(3):
            i = s * 3 + f
            edge_s[0, i:i + 1, :] = wn[s, f, 0:1, :]
            edge_s[1, i:i + 1, :] = wn[s, f, 31:32, :]

    def edge_copy(way):
        return pltpu.make_async_remote_copy(
            src_ref=edge_s.at[way], dst_ref=edge_r.at[way], send_sem=e_send.at[way], recv_sem=e_recv.at[way],
            device_id=(me, (jnp.maximum(sp - 1, 0), jnp.minimum(sp + 1, spaces - 1))[way]), device_id_type=MESH)

    @pl.when(sp > 0)
    def _():
        edge_copy(0).start()

    @pl.when(sp < spaces - 1)
    def _():
        edge_copy(1).start()

    @pl.when(sp < spaces - 1)
    def _():
        edge_copy(0).wait_recv()

    @pl.when(sp > 0)
    def _():
        edge_copy(1).wait_recv()

    tall = lax.broadcasted_iota(jnp.int32, (32, 512), 0)
    for s in range(2):
        w = [wn[s, f] for f in range(3)]
        for f in range(3):
            i = s * 3 + f
            k = kap[f]
            below = jnp.where(tall == 31, edge_r[0, i:i + 1, :], pltpu.roll(w[f], 31, 0))
            above = jnp.where(tall == 0, edge_r[1, i:i + 1, :], pltpu.roll(w[f], 1, 0))
            after = pltpu.roll(w[f], 511, 1)
            before = pltpu.roll(w[f], 1, 1)
            d, e = [n for n in range(3) if n != f]
            res = (0.5 * drift_s[0, f] * (below - above) + 0.5 * drift_s[1, f] * (after - before)
                   - k * (below + above + after + before) + (react_s[f, d] * w[d] + react_s[f, e] * w[e]))
            if s == 0:
                res = res + first_step * (bv[0, f] - (1.0 + 4.0 * k + react_s[f, f]) * out_u[0, f])
            out_res[s, f] = res

    pltpu.make_async_copy(pack.at[some], msgs.at[some], a_send).wait()
    pltpu.make_async_copy(m5.at[some], back5.at[some], r5_send).wait()
    pltpu.make_async_copy(m6.at[some], back6.at[some], r6_send).wait()

    @pl.when(last)
    def _():
        pltpu.make_async_copy(pack.at[some], msgs.at[some], p_send).wait()

    @pl.loop(0, 5)
    def _(j):
        @pl.when(has_up)
        def _():
            row_copy(j, 0).wait_send()

        @pl.when(has_dn)
        def _():
            row_copy(j, 1).wait_send()

        col_copy(j, 0).wait_send()
        col_copy(j, 1).wait_send()

    @pl.when(sp > 0)
    def _():
        edge_copy(0).wait_send()

    @pl.when(sp < spaces - 1)
    def _():
        edge_copy(1).wait_send()


def shards(previous, right_side, kappa, drift, reaction):
    hbm = pl.BlockSpec(memory_space=pltpu.HBM)
    smem = pl.BlockSpec(memory_space=pltpu.SMEM)
    vmem = pl.BlockSpec(memory_space=pltpu.VMEM)
    shape = jax.ShapeDtypeStruct(right_side.shape, F32)
    dma = pltpu.SemaphoreType.DMA
    held = pltpu.VMEM((TM, 3, 8, 128), F32)
    natural = pltpu.VMEM((2, 3, 32, 512), F32)
    return pl.pallas_call(
        kernel,
        out_shape=(shape, shape),
        in_specs=[hbm, hbm, hbm, smem, smem],
        out_specs=(vmem, vmem),
        scratch_shapes=[
            natural,
            pltpu.VMEM((3, 32, 512), F32),
            pltpu.VMEM((3, 32, 512), F32),
            held, held, held,
            pltpu.VMEM((3, 8, 128), F32),
            held, held, held, held, held, held,
            natural,
            pltpu.VMEM((5, 2, 3, 32, 128), F32),
            pltpu.VMEM((5, 2, 3, 32, 128), F32),
            pltpu.VMEM((5, 2, 3, 8, 128), F32),
            pltpu.VMEM((5, 2, 3, 8, 128), F32),
            pltpu.VMEM((2, 8, 512), F32),
            pltpu.VMEM((2, 8, 512), F32),
            pltpu.VMEM((11, 3, 8, 128), F32),
            pltpu.VMEM((2, 3, 32, 128), F32),
            pltpu.VMEM((2, 3, 8, 128), F32),
            dma((4,)),
            dma, dma, dma, dma,
            dma((5, 4)), dma((5, 4)),
            dma, dma, dma, dma,
            dma((2,)), dma((2,)),
        ],
        compiler_params=pltpu.CompilerParams(
            collective_id=0, has_side_effects=True, vmem_limit_bytes=40 * 1024 * 1024),
    )(right_side, previous, kappa, drift.T, reaction)


def solution(mesh):
    in_specs = (
        P("tm", None, "space", None),
        P("tm", None, "space", None),
        P(None, "space", None),
        P(),
        P(),
    )
    out_specs = (P("tm", None, "space", None), P("tm", None, "space", None))
    return jax.shard_map(shards, mesh=mesh, in_specs=in_specs, out_specs=out_specs, check_vma=False)
```

```python
import functools

import jax
import jax.numpy as jnp
from jax import lax
from jax.experimental import pallas as pl
from jax.experimental.pallas import tpu as pltpu
from jax.sharding import PartitionSpec as P

ALPHA = 0.2
TM = 32
MESH = pl.DeviceIdType.MESH
F32 = jnp.float32


def place_of(tile, space):
    r, c = tile // 8, tile % 8
    odd = space % 2
    q = r + odd * (3 - 2 * r)
    half = c // 4
    y = (c % 4) + half * (3 - 2 * (c % 4))
    z = q + half * (7 - 2 * q)
    return y * 8 + z


def tile_of(tm, space):
    y, z = tm // 8, tm % 8
    half = z // 4
    q = z + half * (7 - 2 * z)
    c = half * 4 + y + half * (3 - 2 * y)
    odd = space % 2
    r = q + odd * (3 - 2 * q)
    return r * 8 + c


HOPS = [(dy, dz) for dz in (4, 3, 5, 2, 6, 1, 7, 0) for dy in (2, 1, 3, 0) if (dy, dz) != (0, 0)]
UNROLL = 8


def kernel(
    b_hbm, prev_hbm, kappa_hbm, drift_s, react_s,
    out_u, out_res,
    bv, prev_v, kap, pack, msgs, held, prev_s, prev_r, ua, ub, m5, m6, back5, back6, wn,
    row_s, row_r, col_s, col_r, edge_s, edge_r, edge_n, coef, row_g, col_g,
    in_sem, a_send, a_recv, p_send, p_recv, h_send, h_recv, r5_send, r5_recv, r6_send, r6_recv, e_send, e_recv,
):
    me = lax.axis_index("tm")
    sp = lax.axis_index("space")
    spaces = lax.axis_size("space")
    tile = tile_of(me, sp)
    r, c = tile // 8, tile % 8
    my, mz = me // 8, me % 8
    peers = [((my + dy) % 4) * 8 + (mz + dz) % 8 for dy, dz in HOPS]

    load_b = pltpu.make_async_copy(b_hbm, bv, in_sem.at[0])
    load_k = pltpu.make_async_copy(kappa_hbm, kap, in_sem.at[1])
    load_p = pltpu.make_async_copy(prev_hbm.at[1], prev_v, in_sem.at[2])
    load_b.start()
    load_k.start()
    last = me == TM - 1

    @pl.when(last)
    def _():
        load_p.start()

    row_r[...] = jnp.zeros_like(row_r)
    edge_r[...] = jnp.zeros_like(edge_r)
    edge_s[...] = jnp.zeros_like(edge_s)

    barrier = pltpu.get_barrier_semaphore()
    for p in peers:
        pl.semaphore_signal(barrier, inc=1, device_id=(p, sp), device_id_type=MESH)

    @pl.when(sp > 0)
    def _():
        for n in range(8):
            pl.semaphore_signal(barrier, inc=1, device_id=(place_of(24 + n, sp - 1), sp - 1), device_id_type=MESH)

    @pl.when(sp < spaces - 1)
    def _():
        for n in range(8):
            pl.semaphore_signal(barrier, inc=1, device_id=(place_of(n, sp + 1), sp + 1), device_id_type=MESH)

    edge_up = jnp.logical_and(r == 0, sp > 0)
    edge_dn = jnp.logical_and(r == 3, sp < spaces - 1)

    lane = lax.broadcasted_iota(jnp.int32, (8, 128), 1)
    sub = lax.broadcasted_iota(jnp.int32, (8, 128), 0)
    high = lane >= 64
    inner = lane % 64
    zero = jnp.zeros((8, 128), F32)

    def swap(x):
        return pltpu.roll(x, 64, 1)

    def fold_low(x):
        return jnp.where(high, pltpu.roll(swap(x), 4, 0), x)[0:4]

    def fold_high(x):
        return jnp.where(high, pltpu.roll(x, 4, 0), swap(x))[0:4]

    def unfold(x):
        return jnp.concatenate([x, swap(x)], axis=0)

    load_b.wait()

    @pl.loop(0, 4)
    def _(rr):
        rows = pl.ds(pl.multiple_of(rr * 8, 8), 8)
        for cp in range(4):
            cols = pl.ds(cp * 128, 128)
            for f in range(3):
                first = bv[0, f, rows, cols]
                second = bv[1, f, rows, cols]
                pack[rr * 8 + cp * 2, f] = jnp.where(high, swap(second), first)
                pack[rr * 8 + cp * 2 + 1, f] = jnp.where(high, second, swap(first))

    pl.semaphore_wait(barrier, TM - 1 + jnp.where(edge_up, TM, 0) + jnp.where(edge_dn, TM, 0))

    @pl.when(last)
    def _():
        load_p.wait()

        @pl.loop(0, 4)
        def _(rr):
            rows = pl.ds(pl.multiple_of(rr * 8, 8), 8)
            for cp in range(4):
                for f in range(3):
                    v = prev_v[f, rows, cp * 128:cp * 128 + 128]
                    prev_s[rr * 8 + cp * 2, f] = fold_low(v)
                    prev_s[rr * 8 + cp * 2 + 1, f] = fold_high(v)

        for p in peers:
            pltpu.make_async_remote_copy(
                src_ref=prev_s.at[tile_of(p, sp)], dst_ref=prev_r, send_sem=p_send, recv_sem=p_recv,
                device_id=(p, sp), device_id_type=MESH).start()
        mine = pltpu.make_async_copy(prev_s.at[tile], prev_r, in_sem.at[2])
        mine.start()
        mine.wait()

    for p in peers:
        pltpu.make_async_remote_copy(
            src_ref=pack.at[tile_of(p, sp)], dst_ref=msgs.at[me], send_sem=a_send, recv_sem=a_recv,
            device_id=(p, sp), device_id_type=MESH).start()
    own = pltpu.make_async_copy(pack.at[tile], msgs.at[me], in_sem.at[3])
    own.start()

    load_k.wait()
    rows = pl.ds(pl.multiple_of(r * 8, 8), 8)
    cols = pl.ds(pl.multiple_of((c // 2) * 128, 128), 128)
    upper_half = (c % 2) == 1
    keep = jnp.where(upper_half, lane, 127 - lane) >= 64
    ratio = []
    for f in range(3):
        k = kap[f, rows, cols]
        k = jnp.where(keep, k, swap(k))
        g = 1.0 / (1.0 + 4.0 * k + react_s[f, f])
        ratio.append(g)
        g2 = g * g
        g4 = g2 * g2
        g8 = g4 * g4
        g16 = g8 * g8
        g32 = g16 * g16
        below = g * (0.5 * drift_s[0, f] - k)
        above = g * (-0.5 * drift_s[0, f] - k)
        after = g * (0.5 * drift_s[1, f] - k)
        before = g * (-0.5 * drift_s[1, f] - k)
        d, e = [n for n in range(3) if n != f]
        coef[0, f] = jnp.where(sub == 7, 0.0, below)
        coef[1, f] = jnp.where(sub == 0, 0.0, above)
        coef[2, f] = jnp.where(inner == 63, 0.0, after)
        coef[3, f] = jnp.where(inner == 0, 0.0, before)
        coef[4, f] = g * react_s[f, d]
        coef[5, f] = g * react_s[f, e]
        coef[6, f] = jnp.where(sub == 7, below, jnp.where(sub == 0, above, 0.0))
        coef[7, f] = jnp.where(inner == 63, after, jnp.where(inner == 0, before, 0.0))
        coef[8, f] = g
        coef[9, f] = g32
        coef[10, f] = 1.0 / (1.0 - ALPHA * (g32 * g32))

    def power(i, carry):
        carry = list(carry)
        for u in range(UNROLL):
            m = i * UNROLL + u
            here = inner == m
            for f in range(3):
                w, lft, rgt = carry[3 * f:3 * f + 3]
                row_g[0, f, pl.ds(m, 1), :] = w[0:1]
                row_g[1, f, pl.ds(m, 1), :] = w[7:8]
                lft = jnp.where(here, pltpu.roll(w, m, 1), lft)
                rgt = jnp.where(here, pltpu.roll(w, m + 65, 1), rgt)
                carry[3 * f:3 * f + 3] = [w * coef[8, f], lft, rgt]
        return tuple(carry)

    start = []
    for f in range(3):
        start += [ratio[f], zero, zero]
    ends = lax.fori_loop(0, 32 // UNROLL, power, tuple(start))
    for f in range(3):
        col_g[0, f] = ends[3 * f + 1]
        col_g[1, f] = ends[3 * f + 2]

    left = place_of(r * 8 + (c + 7) % 8, sp)
    right = place_of(r * 8 + (c + 1) % 8, sp)
    up_in = r > 0
    dn_in = r < 3
    has_up = jnp.logical_or(up_in, sp > 0)
    has_dn = jnp.logical_or(dn_in, sp < spaces - 1)
    up_tm = jnp.where(up_in, place_of(jnp.maximum(r - 1, 0) * 8 + c, sp), me)
    up_sp = jnp.where(up_in, sp, jnp.maximum(sp - 1, 0))
    dn_tm = jnp.where(dn_in, place_of(jnp.minimum(r + 1, 3) * 8 + c, sp), me)
    dn_sp = jnp.where(dn_in, sp, jnp.minimum(sp + 1, spaces - 1))

    def row_copy(j, way):
        return pltpu.make_async_remote_copy(
            src_ref=row_s.at[j, way], dst_ref=row_r.at[j, way], send_sem=h_send.at[j, way], recv_sem=h_recv.at[j, way],
            device_id=((up_tm, up_sp), (dn_tm, dn_sp))[way], device_id_type=MESH)

    def col_copy(j, way):
        return pltpu.make_async_remote_copy(
            src_ref=col_s.at[j, way], dst_ref=col_r.at[j, way], send_sem=h_send.at[j, 2 + way],
            recv_sem=h_recv.at[j, 2 + way], device_id=((left, right)[way], sp), device_id_type=MESH)

    def carry_in(ends):
        out = []
        for f in range(3):
            end, other = ends[f], swap(ends[f])
            g32 = coef[9, f]
            final = (jnp.where(high, end, other) + g32 * jnp.where(high, other, end)) * coef[10, f]
            wrap = ALPHA * final
            out.append(jnp.where(high, other + g32 * wrap, wrap))
        return out

    def send_halo(j, came, lefts, rights):
        for f in range(3):
            col_s[j, 0, f] = lefts[f] + col_g[0, f] * jnp.where(high, came[f][:, 64:65], came[f][:, 0:1])
            col_s[j, 1, f] = rights[f] + col_g[1, f] * jnp.where(high, came[f][:, 127:128], came[f][:, 63:64])
        col_copy(j, 0).start()
        col_copy(j, 1).start()
        for f in range(3):
            row_s[j, 0, f] = row_s[j, 0, f] + row_g[0, f] * came[f][0:1]
            row_s[j, 1, f] = row_s[j, 1, f] + row_g[1, f] * came[f][7:8]

        @pl.when(has_up)
        def _():
            row_copy(j, 0).start()

        @pl.when(has_dn)
        def _():
            row_copy(j, 1).start()

    def await_halo(j):
        @pl.when(has_dn)
        def _():
            row_copy(j, 0).wait_recv()

        @pl.when(has_up)
        def _():
            row_copy(j, 1).wait_recv()

        col_copy(j, 0).wait_recv()
        col_copy(j, 1).wait_recv()

    def pack_border(j, m, f, u, lft, rgt):
        here = inner == m
        row_s[j, 0, f, pl.ds(m, 1), :] = u[0:1]
        row_s[j, 1, f, pl.ds(m, 1), :] = u[7:8]
        return jnp.where(here, pltpu.roll(u, m, 1), lft), jnp.where(here, pltpu.roll(u, m + 65, 1), rgt)

    def interior(came, src, dst):
        def step(i, carry):
            carry = list(carry)
            for u in range(UNROLL):
                m = i * UNROLL + u
                v = []
                for f in range(3):
                    carry[f] = carry[f] * coef[8, f]
                    v.append(src[m, f] + carry[f])
                    if dst is not src:
                        src[m, f] = v[f]
                for f in range(3):
                    d, e = [n for n in range(3) if n != f]
                    off = (coef[0, f] * pltpu.roll(v[f], 7, 0) + coef[1, f] * pltpu.roll(v[f], 1, 0)
                           + coef[2, f] * pltpu.roll(v[f], 127, 1) + coef[3, f] * pltpu.roll(v[f], 1, 1)
                           + coef[4, f] * v[d] + coef[5, f] * v[e])
                    dst[m, f] = held[m, f] - off
            return tuple(carry)

        lax.fori_loop(0, 32 // UNROLL, step, tuple(came))

    def border_scan(j, dst, halo):
        def step(i, carry):
            carry = list(carry)
            for u in range(UNROLL):
                m = i * UNROLL + u
                for f in range(3):
                    before, lft, rgt = carry[3 * f:3 * f + 3]
                    rows = jnp.where(sub == 0, row_r[j, 1, f, pl.ds(m, 1), :], row_r[j, 0, f, pl.ds(m, 1), :])
                    cols = jnp.where(inner == 0, pltpu.roll(col_r[j, 1, f], (128 - m) % 128, 1),
                                     pltpu.roll(col_r[j, 0, f], 63 - m, 1))
                    x = dst[m, f] - (coef[6, f] * rows + coef[7, f] * cols)
                    now = x + coef[8, f] * before
                    dst[m, f] = now
                    if halo:
                        lft, rgt = pack_border(j + 1, m, f, now, lft, rgt)
                    carry[3 * f:3 * f + 3] = [now, lft, rgt]
            return tuple(carry)

        ends = lax.fori_loop(0, 32 // UNROLL, step, (zero,) * 9)
        return ends[0::3], ends[1::3], ends[2::3]

    own.wait()
    some = pl.ds(0, TM - 1)
    pltpu.make_async_copy(pack.at[some], msgs.at[some], a_recv).wait()

    @pl.when(jnp.logical_not(last))
    def _():
        pltpu.make_async_copy(prev_r, prev_r, p_recv).wait()

    for f in range(3):
        p = unfold(prev_r[f])
        msgs[0, f] = msgs[0, f] - ALPHA * jnp.where(high, 0.0, p)

    def first(i, carry):
        carry = list(carry)
        for u in range(UNROLL // 2):
            h = i * (UNROLL // 2) + u
            for f in range(3):
                before, lft, rgt = carry[3 * f:3 * f + 3]
                g = coef[8, f]
                a, b = msgs[h, f], msgs[16 + h, f]
                even = g * jnp.where(high, swap(b), a)
                odd = g * jnp.where(high, b, swap(a))
                held[2 * h, f] = even
                held[2 * h + 1, f] = odd
                now = even + g * before
                ua[2 * h, f] = now
                lft, rgt = pack_border(0, 2 * h, f, now, lft, rgt)
                now = odd + g * now
                ua[2 * h + 1, f] = now
                lft, rgt = pack_border(0, 2 * h + 1, f, now, lft, rgt)
                carry[3 * f:3 * f + 3] = [now, lft, rgt]
        return tuple(carry)

    ends = lax.fori_loop(0, 32 // UNROLL, first, (zero,) * 9)
    came = carry_in(ends[0::3])
    send_halo(0, came, ends[1::3], ends[2::3])

    def sweep(j, came):
        interior(came, ua, ua)
        await_halo(j)
        ends, lefts, rights = border_scan(j, ua, True)
        came = carry_in(ends)
        send_halo(j + 1, came, lefts, rights)
        return tuple(came)

    came = lax.fori_loop(0, 4, sweep, tuple(came))

    def fold_even(i, carry):
        for u in range(UNROLL // 2):
            h = i * (UNROLL // 2) + u
            for f in range(3):
                even = ua[2 * h, f]
                m5[h, f] = fold_low(even)
                m5[16 + h, f] = fold_high(even)
        return carry

    def to_messages(i, carry):
        carry = list(carry)
        for u in range(UNROLL // 2):
            h = i * (UNROLL // 2) + u
            for f in range(3):
                w = carry[f] * coef[8, f]
                even = ub[2 * h, f] + w
                w = w * coef[8, f]
                odd = ub[2 * h + 1, f] + w
                carry[f] = w
                fifth = ua[2 * h, f]
                one = jnp.where(high, swap(odd), even)
                two = jnp.where(high, odd, swap(even))
                m6[h, f] = one
                m6[16 + h, f] = two
                one = jnp.where(high, 0.0, fifth) * jnp.where(h == 0, 0.0, 1.0) - one
                two = jnp.where(high, 0.0, swap(fifth)) - two
                edge_s[h, f:f + 1, :] = jnp.where(r == 0, one[0:1], one[7:8])
                edge_s[16 + h, f:f + 1, :] = jnp.where(r == 0, two[0:1], two[7:8])
        return tuple(carry)

    def send_back(src, dst, send_sem, recv_sem, own_sem):
        for p in peers:
            pltpu.make_async_remote_copy(
                src_ref=src.at[p], dst_ref=dst.at[tile], send_sem=send_sem, recv_sem=recv_sem,
                device_id=(p, sp), device_id_type=MESH).start()
        own = pltpu.make_async_copy(src.at[me], dst.at[tile], own_sem)
        own.start()
        return own

    interior(came, ua, ub)
    lax.fori_loop(0, 32 // UNROLL, fold_even, 0)
    own5 = send_back(m5, back5, r5_send, r5_recv, in_sem.at[0])
    await_halo(4)
    ends, _, _ = border_scan(4, ub, False)
    lax.fori_loop(0, 32 // UNROLL, to_messages, tuple(carry_in(ends)))
    own6 = send_back(m6, back6, r6_send, r6_recv, in_sem.at[1])

    def send_edge(way):
        for o in range(TM):
            p = (me + o) % TM
            pltpu.make_async_remote_copy(
                src_ref=edge_s.at[p], dst_ref=edge_r.at[way, c], send_sem=e_send, recv_sem=e_recv.at[way],
                device_id=(p, sp - 1 + 2 * way), device_id_type=MESH).start()

    @pl.when(edge_up)
    def _():
        send_edge(0)

    @pl.when(edge_dn)
    def _():
        send_edge(1)

    own5.wait()
    own6.wait()
    pltpu.make_async_copy(m5.at[some], back5.at[some], r5_recv).wait()
    pltpu.make_async_copy(m6.at[some], back6.at[some], r6_recv).wait()

    first_step = jnp.where(me == 0, 1.0, 0.0)

    @pl.loop(0, 4)
    def _(rr):
        rows = pl.ds(pl.multiple_of(rr * 8, 8), 8)
        for cp in range(4):
            cols = pl.ds(cp * 128, 128)
            t = rr * 8 + cp * 2
            for f in range(3):
                a6, b6 = back6[t, f], back6[t + 1, f]
                n0 = jnp.where(high, swap(b6), a6)
                n1 = jnp.where(high, b6, swap(a6))
                o0 = jnp.where(high, swap(unfold(back5[t + 1, f])), unfold(back5[t, f]))
                out_u[0, f, rows, cols] = n0
                out_u[1, f, rows, cols] = n1
                wn[0, f, rows, cols] = o0 * (1.0 - first_step) - n0
                wn[1, f, rows, cols] = -n1

    @pl.when(sp < spaces - 1)
    def _():
        pltpu.make_async_copy(edge_r.at[0], edge_r.at[0], e_recv.at[0]).wait()

    @pl.when(sp > 0)
    def _():
        pltpu.make_async_copy(edge_r.at[1], edge_r.at[1], e_recv.at[1]).wait()

    high4 = lax.broadcasted_iota(jnp.int32, (4, 128), 1) >= 64
    for way in range(2):
        for cp in range(4):
            a, b = edge_r[way, 2 * cp], edge_r[way, 2 * cp + 1]
            edge_n[way, 0, :, cp * 128:cp * 128 + 128] = jnp.where(high4, swap(b), a)
            edge_n[way, 1, :, cp * 128:cp * 128 + 128] = jnp.where(high4, b, swap(a))

    tall = lax.broadcasted_iota(jnp.int32, (32, 512), 0)
    for s in range(2):
        w = [wn[s, f] for f in range(3)]
        for f in range(3):
            k = kap[f]
            below = jnp.where(tall == 31, edge_n[0, s, f:f + 1, :], pltpu.roll(w[f], 31, 0))
            above = jnp.where(tall == 0, edge_n[1, s, f:f + 1, :], pltpu.roll(w[f], 1, 0))
            after = pltpu.roll(w[f], 511, 1)
            before = pltpu.roll(w[f], 1, 1)
            d, e = [n for n in range(3) if n != f]
            res = (0.5 * drift_s[0, f] * (below - above) + 0.5 * drift_s[1, f] * (after - before)
                   - k * (below + above + after + before) + (react_s[f, d] * w[d] + react_s[f, e] * w[e]))
            own = bv[s, f] - (1.0 + 4.0 * k + react_s[f, f]) * out_u[s, f]
            if s == 0:
                res = res + first_step * own
            else:
                res = res + (own + out_u[0, f])
            out_res[s, f] = res

    pltpu.make_async_copy(pack.at[some], msgs.at[some], a_send).wait()
    pltpu.make_async_copy(m5.at[some], back5.at[some], r5_send).wait()
    pltpu.make_async_copy(m6.at[some], back6.at[some], r6_send).wait()

    @pl.when(last)
    def _():
        pltpu.make_async_copy(prev_s.at[some], prev_s.at[some], p_send).wait()

    @pl.loop(0, 5)
    def _(j):
        @pl.when(has_up)
        def _():
            row_copy(j, 0).wait_send()

        @pl.when(has_dn)
        def _():
            row_copy(j, 1).wait_send()

        col_copy(j, 0).wait_send()
        col_copy(j, 1).wait_send()

    @pl.when(jnp.logical_or(edge_up, edge_dn))
    def _():
        pltpu.make_async_copy(edge_s, edge_s, e_send).wait()


def shards(previous, right_side, kappa, drift, reaction):
    hbm = pl.BlockSpec(memory_space=pltpu.HBM)
    smem = pl.BlockSpec(memory_space=pltpu.SMEM)
    vmem = pl.BlockSpec(memory_space=pltpu.VMEM)
    shape = jax.ShapeDtypeStruct(right_side.shape, F32)
    dma = pltpu.SemaphoreType.DMA
    held = pltpu.VMEM((TM, 3, 8, 128), F32)
    folded = pltpu.VMEM((TM, 3, 4, 128), F32)
    natural = pltpu.VMEM((2, 3, 32, 512), F32)
    return pl.pallas_call(
        kernel,
        out_shape=(shape, shape),
        in_specs=[hbm, hbm, hbm, smem, smem],
        out_specs=(vmem, vmem),
        scratch_shapes=[
            natural,
            pltpu.VMEM((3, 32, 512), F32),
            pltpu.VMEM((3, 32, 512), F32),
            held, held, held,
            folded, pltpu.VMEM((3, 4, 128), F32),
            held, held, folded, held, folded, held,
            natural,
            pltpu.VMEM((5, 2, 3, 32, 128), F32),
            pltpu.VMEM((5, 2, 3, 32, 128), F32),
            pltpu.VMEM((5, 2, 3, 8, 128), F32),
            pltpu.VMEM((5, 2, 3, 8, 128), F32),
            pltpu.VMEM((TM, 4, 128), F32),
            pltpu.VMEM((2, 8, 4, 128), F32),
            pltpu.VMEM((2, 2, 4, 512), F32),
            pltpu.VMEM((11, 3, 8, 128), F32),
            pltpu.VMEM((2, 3, 32, 128), F32),
            pltpu.VMEM((2, 3, 8, 128), F32),
            dma((4,)),
            dma, dma, dma, dma,
            dma((5, 4)), dma((5, 4)),
            dma, dma, dma, dma,
            dma, dma((2,)),
        ],
        compiler_params=pltpu.CompilerParams(
            collective_id=0, has_side_effects=True, vmem_limit_bytes=56 * 1024 * 1024),
    )(right_side, previous, kappa, drift.T, reaction)


def solution(mesh):
    in_specs = (
        P("tm", None, "space", None),
        P("tm", None, "space", None),
        P(None, "space", None),
        P(),
        P(),
    )
    out_specs = (P("tm", None, "space", None), P("tm", None, "space", None))
    return jax.shard_map(shards, mesh=mesh, in_specs=in_specs, out_specs=out_specs, check_vma=False)
```

```python
import functools

import jax
import jax.numpy as jnp
from jax import lax
from jax.experimental import pallas as pl
from jax.experimental.pallas import tpu as pltpu
from jax.sharding import PartitionSpec as P

ALPHA = 0.2
TM = 32
MESH = pl.DeviceIdType.MESH
F32 = jnp.float32


div, rem = lax.div, lax.rem


def place_of(r, c, odd):
    q = r + odd * (3 - 2 * r)
    half, y = div(c, 4), rem(c, 4)
    y = y + half * (3 - 2 * y)
    return y * 8 + q + half * (7 - 2 * q)


def tile_of(y, z, odd):
    half = div(z, 4)
    q = z + half * (7 - 2 * z)
    c = half * 4 + y + half * (3 - 2 * y)
    return (q + odd * (3 - 2 * q)) * 8 + c


HOPS = [(dy, dz) for dz in (4, 3, 5, 2, 6, 1, 7, 0) for dy in (2, 1, 3, 0) if (dy, dz) != (0, 0)]
UNROLL = 8


def kernel(
    b_hbm, prev_hbm, kappa_hbm, drift_s, react_s,
    out_u, out_res,
    bv, prev_v, kap, pack, msgs, held, prev_s, prev_r, ua, ub, m5, m6, back5, back6, wn,
    row_s, row_r, col_s, col_r, edge_s, edge_r, edge_n, coef, row_g, col_g,
    in_sem, a_send, a_recv, p_send, p_recv, h_send, h_recv, r5_send, r5_recv, r6_send, r6_recv, e_send, e_recv, ready,
):
    me = lax.axis_index("tm")
    sp = lax.axis_index("space")
    spaces = lax.axis_size("space")
    my, mz, odd_space = div(me, 8), rem(me, 8), rem(sp, 2)
    tile = tile_of(my, mz, odd_space)
    r, c = div(tile, 8), rem(tile, 8)
    places = [(rem(my + dy, 4), rem(mz + dz, 8)) for dy, dz in HOPS]
    peers = [y * 8 + z for y, z in places]

    load_b = pltpu.make_async_copy(b_hbm, bv, in_sem.at[0])
    load_k = pltpu.make_async_copy(kappa_hbm, kap, in_sem.at[1])
    load_p = pltpu.make_async_copy(prev_hbm.at[1], prev_v, in_sem.at[2])
    load_b.start()
    load_k.start()
    last = me == TM - 1

    @pl.when(last)
    def _():
        load_p.start()

    row_r[...] = jnp.zeros_like(row_r)
    edge_r[...] = jnp.zeros_like(edge_r)
    edge_s[...] = jnp.zeros_like(edge_s)

    barrier = pltpu.get_barrier_semaphore()
    for p in peers:
        pl.semaphore_signal(barrier, inc=1, device_id=(p, sp), device_id_type=MESH)

    @pl.when(sp > 0)
    def _():
        pl.semaphore_signal(barrier, inc=1, device_id=(me, sp - 1), device_id_type=MESH)

    @pl.when(sp < spaces - 1)
    def _():
        pl.semaphore_signal(barrier, inc=1, device_id=(me, sp + 1), device_id_type=MESH)

    edge_up = jnp.logical_and(r == 0, sp > 0)
    edge_dn = jnp.logical_and(r == 3, sp < spaces - 1)

    lane = lax.broadcasted_iota(jnp.int32, (8, 128), 1)
    sub = lax.broadcasted_iota(jnp.int32, (8, 128), 0)
    high = lane >= 64
    inner = lane % 64
    zero = jnp.zeros((8, 128), F32)

    def swap(x):
        return pltpu.roll(x, 64, 1)

    def fold_low(x):
        return jnp.where(high, pltpu.roll(swap(x), 4, 0), x)[0:4]

    def fold_high(x):
        return jnp.where(high, pltpu.roll(x, 4, 0), swap(x))[0:4]

    def unfold(x):
        return jnp.concatenate([x, swap(x)], axis=0)

    load_b.wait()

    @pl.loop(0, 4)
    def _(rr):
        rows = pl.ds(pl.multiple_of(rr * 8, 8), 8)
        for cp in range(4):
            cols = pl.ds(cp * 128, 128)
            for f in range(3):
                first = bv[0, f, rows, cols]
                second = bv[1, f, rows, cols]
                pack[rr * 8 + cp * 2, f] = jnp.where(high, swap(second), first)
                pack[rr * 8 + cp * 2 + 1, f] = jnp.where(high, second, swap(first))

    pl.semaphore_wait(barrier, TM - 1 + jnp.where(sp > 0, 1, 0) + jnp.where(sp < spaces - 1, 1, 0))

    @pl.when(last)
    def _():
        load_p.wait()

        @pl.loop(0, 4)
        def _(rr):
            rows = pl.ds(pl.multiple_of(rr * 8, 8), 8)
            for cp in range(4):
                for f in range(3):
                    v = prev_v[f, rows, cp * 128:cp * 128 + 128]
                    prev_s[rr * 8 + cp * 2, f] = fold_low(v)
                    prev_s[rr * 8 + cp * 2 + 1, f] = fold_high(v)

        for p, (y, z) in zip(peers, places):
            pltpu.make_async_remote_copy(
                src_ref=prev_s.at[tile_of(y, z, odd_space)], dst_ref=prev_r, send_sem=p_send, recv_sem=p_recv,
                device_id=(p, sp), device_id_type=MESH).start()
        mine = pltpu.make_async_copy(prev_s.at[tile], prev_r, in_sem.at[2])
        mine.start()
        mine.wait()

    for p, (y, z) in zip(peers, places):
        pltpu.make_async_remote_copy(
            src_ref=pack.at[tile_of(y, z, odd_space)], dst_ref=msgs.at[me], send_sem=a_send, recv_sem=a_recv,
            device_id=(p, sp), device_id_type=MESH).start()
    own = pltpu.make_async_copy(pack.at[tile], msgs.at[me], in_sem.at[3])
    own.start()

    load_k.wait()
    rows = pl.ds(pl.multiple_of(r * 8, 8), 8)
    cols = pl.ds(pl.multiple_of(div(c, 2) * 128, 128), 128)
    upper_half = rem(c, 2) == 1
    keep = jnp.where(upper_half, lane, 127 - lane) >= 64
    ratio = []
    for f in range(3):
        k = kap[f, rows, cols]
        k = jnp.where(keep, k, swap(k))
        g = 1.0 / (1.0 + 4.0 * k + react_s[f, f])
        ratio.append(g)
        g2 = g * g
        g4 = g2 * g2
        g8 = g4 * g4
        g16 = g8 * g8
        g32 = g16 * g16
        below = g * (0.5 * drift_s[0, f] - k)
        above = g * (-0.5 * drift_s[0, f] - k)
        after = g * (0.5 * drift_s[1, f] - k)
        before = g * (-0.5 * drift_s[1, f] - k)
        d, e = [n for n in range(3) if n != f]
        coef[0, f] = jnp.where(sub == 7, 0.0, below)
        coef[1, f] = jnp.where(sub == 0, 0.0, above)
        coef[2, f] = jnp.where(inner == 63, 0.0, after)
        coef[3, f] = jnp.where(inner == 0, 0.0, before)
        coef[4, f] = g * react_s[f, d]
        coef[5, f] = g * react_s[f, e]
        coef[6, f] = jnp.where(sub == 7, below, jnp.where(sub == 0, above, 0.0))
        coef[7, f] = jnp.where(inner == 63, after, jnp.where(inner == 0, before, 0.0))
        coef[8, f] = g
        coef[9, f] = g32
        coef[10, f] = 1.0 / (1.0 - ALPHA * (g32 * g32))

    def power(i, carry):
        carry = list(carry)
        for u in range(UNROLL):
            m = i * UNROLL + u
            here = inner == m
            for f in range(3):
                w, lft, rgt = carry[3 * f:3 * f + 3]
                row_g[0, f, pl.ds(m, 1), :] = w[0:1]
                row_g[1, f, pl.ds(m, 1), :] = w[7:8]
                lft = jnp.where(here, pltpu.roll(w, m, 1), lft)
                rgt = jnp.where(here, pltpu.roll(w, m + 65, 1), rgt)
                carry[3 * f:3 * f + 3] = [w * coef[8, f], lft, rgt]
        return tuple(carry)

    start = []
    for f in range(3):
        start += [ratio[f], zero, zero]
    ends = lax.fori_loop(0, 32 // UNROLL, power, tuple(start))
    for f in range(3):
        col_g[0, f] = ends[3 * f + 1]
        col_g[1, f] = ends[3 * f + 2]

    left = place_of(r, rem(c + 7, 8), odd_space)
    right = place_of(r, rem(c + 1, 8), odd_space)
    up_in = r > 0
    dn_in = r < 3
    has_up = jnp.logical_or(up_in, sp > 0)
    has_dn = jnp.logical_or(dn_in, sp < spaces - 1)
    up_tm = jnp.where(up_in, place_of(jnp.maximum(r - 1, 0), c, odd_space), me)
    up_sp = jnp.where(up_in, sp, jnp.maximum(sp - 1, 0))
    dn_tm = jnp.where(dn_in, place_of(jnp.minimum(r + 1, 3), c, odd_space), me)
    dn_sp = jnp.where(dn_in, sp, jnp.minimum(sp + 1, spaces - 1))

    def row_copy(j, way):
        return pltpu.make_async_remote_copy(
            src_ref=row_s.at[j, way], dst_ref=row_r.at[j, way], send_sem=h_send.at[j, way], recv_sem=h_recv.at[j, way],
            device_id=((up_tm, up_sp), (dn_tm, dn_sp))[way], device_id_type=MESH)

    def col_copy(j, way):
        return pltpu.make_async_remote_copy(
            src_ref=col_s.at[j, way], dst_ref=col_r.at[j, way], send_sem=h_send.at[j, 2 + way],
            recv_sem=h_recv.at[j, 2 + way], device_id=((left, right)[way], sp), device_id_type=MESH)

    def carry_in(ends):
        out = []
        for f in range(3):
            end, other = ends[f], swap(ends[f])
            g32 = coef[9, f]
            final = (jnp.where(high, end, other) + g32 * jnp.where(high, other, end)) * coef[10, f]
            wrap = ALPHA * final
            out.append(jnp.where(high, other + g32 * wrap, wrap))
        return out

    def send_halo(j, came, lefts, rights):
        for f in range(3):
            col_s[j, 0, f] = lefts[f] + col_g[0, f] * jnp.where(high, came[f][:, 64:65], came[f][:, 0:1])
            col_s[j, 1, f] = rights[f] + col_g[1, f] * jnp.where(high, came[f][:, 127:128], came[f][:, 63:64])
        col_copy(j, 0).start()
        col_copy(j, 1).start()
        for f in range(3):
            row_s[j, 0, f] = row_s[j, 0, f] + row_g[0, f] * came[f][0:1]
            row_s[j, 1, f] = row_s[j, 1, f] + row_g[1, f] * came[f][7:8]

        @pl.when(has_up)
        def _():
            row_copy(j, 0).start()

        @pl.when(has_dn)
        def _():
            row_copy(j, 1).start()

    def await_halo(j):
        @pl.when(has_dn)
        def _():
            row_copy(j, 0).wait_recv()

        @pl.when(has_up)
        def _():
            row_copy(j, 1).wait_recv()

        col_copy(j, 0).wait_recv()
        col_copy(j, 1).wait_recv()

    def pack_border(j, m, f, u, lft, rgt):
        here = inner == m
        row_s[j, 0, f, pl.ds(m, 1), :] = u[0:1]
        row_s[j, 1, f, pl.ds(m, 1), :] = u[7:8]
        return jnp.where(here, pltpu.roll(u, m, 1), lft), jnp.where(here, pltpu.roll(u, m + 65, 1), rgt)

    def interior(came, src, dst):
        def step(i, carry):
            carry = list(carry)
            for u in range(UNROLL):
                m = i * UNROLL + u
                v = []
                for f in range(3):
                    carry[f] = carry[f] * coef[8, f]
                    v.append(src[m, f] + carry[f])
                    if dst is not src:
                        src[m, f] = v[f]
                for f in range(3):
                    d, e = [n for n in range(3) if n != f]
                    off = (coef[0, f] * pltpu.roll(v[f], 7, 0) + coef[1, f] * pltpu.roll(v[f], 1, 0)
                           + coef[2, f] * pltpu.roll(v[f], 127, 1) + coef[3, f] * pltpu.roll(v[f], 1, 1)
                           + coef[4, f] * v[d] + coef[5, f] * v[e])
                    dst[m, f] = held[m, f] - off
            return tuple(carry)

        lax.fori_loop(0, 32 // UNROLL, step, tuple(came))

    def border_scan(j, dst, halo):
        def step(i, carry):
            carry = list(carry)
            for u in range(UNROLL):
                m = i * UNROLL + u
                for f in range(3):
                    before, lft, rgt = carry[3 * f:3 * f + 3]
                    rows = jnp.where(sub == 0, row_r[j, 1, f, pl.ds(m, 1), :], row_r[j, 0, f, pl.ds(m, 1), :])
                    cols = jnp.where(inner == 0, pltpu.roll(col_r[j, 1, f], rem(128 - m, 128), 1),
                                     pltpu.roll(col_r[j, 0, f], 63 - m, 1))
                    x = dst[m, f] - (coef[6, f] * rows + coef[7, f] * cols)
                    now = x + coef[8, f] * before
                    dst[m, f] = now
                    if halo:
                        lft, rgt = pack_border(j + 1, m, f, now, lft, rgt)
                    carry[3 * f:3 * f + 3] = [now, lft, rgt]
            return tuple(carry)

        ends = lax.fori_loop(0, 32 // UNROLL, step, (zero,) * 9)
        return ends[0::3], ends[1::3], ends[2::3]

    own.wait()
    some = pl.ds(0, TM - 1)
    pltpu.make_async_copy(pack.at[some], msgs.at[some], a_recv).wait()

    @pl.when(jnp.logical_not(last))
    def _():
        pltpu.make_async_copy(prev_r, prev_r, p_recv).wait()

    for f in range(3):
        p = unfold(prev_r[f])
        msgs[0, f] = msgs[0, f] - ALPHA * jnp.where(high, 0.0, p)

    def first(i, carry):
        carry = list(carry)
        for u in range(UNROLL // 2):
            h = i * (UNROLL // 2) + u
            for f in range(3):
                before, lft, rgt = carry[3 * f:3 * f + 3]
                g = coef[8, f]
                a, b = msgs[h, f], msgs[16 + h, f]
                even = g * jnp.where(high, swap(b), a)
                odd = g * jnp.where(high, b, swap(a))
                held[2 * h, f] = even
                held[2 * h + 1, f] = odd
                now = even + g * before
                ua[2 * h, f] = now
                lft, rgt = pack_border(0, 2 * h, f, now, lft, rgt)
                now = odd + g * now
                ua[2 * h + 1, f] = now
                lft, rgt = pack_border(0, 2 * h + 1, f, now, lft, rgt)
                carry[3 * f:3 * f + 3] = [now, lft, rgt]
        return tuple(carry)

    ends = lax.fori_loop(0, 32 // UNROLL, first, (zero,) * 9)
    came = carry_in(ends[0::3])
    send_halo(0, came, ends[1::3], ends[2::3])

    @pl.when(sp > 0)
    def _():
        for n in range(8):
            pl.semaphore_signal(
                ready, inc=1, device_id=(place_of(3, jnp.int32(n), 1 - odd_space), sp - 1), device_id_type=MESH)

    @pl.when(sp < spaces - 1)
    def _():
        for n in range(8):
            pl.semaphore_signal(
                ready, inc=1, device_id=(place_of(0, jnp.int32(n), 1 - odd_space), sp + 1), device_id_type=MESH)

    def sweep(j, came):
        interior(came, ua, ua)
        await_halo(j)
        ends, lefts, rights = border_scan(j, ua, True)
        came = carry_in(ends)
        send_halo(j + 1, came, lefts, rights)
        return tuple(came)

    came = lax.fori_loop(0, 4, sweep, tuple(came))

    def fold_even(i, carry):
        for u in range(UNROLL // 2):
            h = i * (UNROLL // 2) + u
            for f in range(3):
                even = ua[2 * h, f]
                m5[h, f] = fold_low(even)
                m5[16 + h, f] = fold_high(even)
        return carry

    def to_messages(i, carry):
        carry = list(carry)
        for u in range(UNROLL // 2):
            h = i * (UNROLL // 2) + u
            for f in range(3):
                w = carry[f] * coef[8, f]
                even = ub[2 * h, f] + w
                w = w * coef[8, f]
                odd = ub[2 * h + 1, f] + w
                carry[f] = w
                fifth = ua[2 * h, f]
                one = jnp.where(high, swap(odd), even)
                two = jnp.where(high, odd, swap(even))
                m6[h, f] = one
                m6[16 + h, f] = two
                one = jnp.where(high, 0.0, fifth) * jnp.where(h == 0, 0.0, 1.0) - one
                two = jnp.where(high, 0.0, swap(fifth)) - two
                edge_s[h, f:f + 1, :] = jnp.where(r == 0, one[0:1], one[7:8])
                edge_s[16 + h, f:f + 1, :] = jnp.where(r == 0, two[0:1], two[7:8])
        return tuple(carry)

    def send_back(src, dst, send_sem, recv_sem, own_sem):
        for p in peers:
            pltpu.make_async_remote_copy(
                src_ref=src.at[p], dst_ref=dst.at[tile], send_sem=send_sem, recv_sem=recv_sem,
                device_id=(p, sp), device_id_type=MESH).start()
        own = pltpu.make_async_copy(src.at[me], dst.at[tile], own_sem)
        own.start()
        return own

    interior(came, ua, ub)
    lax.fori_loop(0, 32 // UNROLL, fold_even, 0)
    own5 = send_back(m5, back5, r5_send, r5_recv, in_sem.at[0])
    await_halo(4)
    ends, _, _ = border_scan(4, ub, False)
    lax.fori_loop(0, 32 // UNROLL, to_messages, tuple(carry_in(ends)))
    own6 = send_back(m6, back6, r6_send, r6_recv, in_sem.at[1])

    def send_edge(way):
        pl.semaphore_wait(ready, TM)
        for o in range(TM):
            p = rem(me + o, TM)
            pltpu.make_async_remote_copy(
                src_ref=edge_s.at[p], dst_ref=edge_r.at[way, c], send_sem=e_send, recv_sem=e_recv.at[way],
                device_id=(p, sp - 1 + 2 * way), device_id_type=MESH).start()

    @pl.when(edge_up)
    def _():
        send_edge(0)

    @pl.when(edge_dn)
    def _():
        send_edge(1)

    own5.wait()
    own6.wait()
    pltpu.make_async_copy(m5.at[some], back5.at[some], r5_recv).wait()
    pltpu.make_async_copy(m6.at[some], back6.at[some], r6_recv).wait()

    first_step = jnp.where(me == 0, 1.0, 0.0)

    @pl.loop(0, 4)
    def _(rr):
        rows = pl.ds(pl.multiple_of(rr * 8, 8), 8)
        for cp in range(4):
            cols = pl.ds(cp * 128, 128)
            t = rr * 8 + cp * 2
            for f in range(3):
                a6, b6 = back6[t, f], back6[t + 1, f]
                n0 = jnp.where(high, swap(b6), a6)
                n1 = jnp.where(high, b6, swap(a6))
                o0 = jnp.where(high, swap(unfold(back5[t + 1, f])), unfold(back5[t, f]))
                out_u[0, f, rows, cols] = n0
                out_u[1, f, rows, cols] = n1
                wn[0, f, rows, cols] = o0 * (1.0 - first_step) - n0
                wn[1, f, rows, cols] = -n1

    @pl.when(sp < spaces - 1)
    def _():
        pltpu.make_async_copy(edge_r.at[0], edge_r.at[0], e_recv.at[0]).wait()

    @pl.when(sp > 0)
    def _():
        pltpu.make_async_copy(edge_r.at[1], edge_r.at[1], e_recv.at[1]).wait()

    high4 = lax.broadcasted_iota(jnp.int32, (4, 128), 1) >= 64
    for way in range(2):
        for cp in range(4):
            a, b = edge_r[way, 2 * cp], edge_r[way, 2 * cp + 1]
            edge_n[way, 0, :, cp * 128:cp * 128 + 128] = jnp.where(high4, swap(b), a)
            edge_n[way, 1, :, cp * 128:cp * 128 + 128] = jnp.where(high4, b, swap(a))

    tall = lax.broadcasted_iota(jnp.int32, (32, 512), 0)
    for s in range(2):
        w = [wn[s, f] for f in range(3)]
        for f in range(3):
            k = kap[f]
            below = jnp.where(tall == 31, edge_n[0, s, f:f + 1, :], pltpu.roll(w[f], 31, 0))
            above = jnp.where(tall == 0, edge_n[1, s, f:f + 1, :], pltpu.roll(w[f], 1, 0))
            after = pltpu.roll(w[f], 511, 1)
            before = pltpu.roll(w[f], 1, 1)
            d, e = [n for n in range(3) if n != f]
            res = (0.5 * drift_s[0, f] * (below - above) + 0.5 * drift_s[1, f] * (after - before)
                   - k * (below + above + after + before) + (react_s[f, d] * w[d] + react_s[f, e] * w[e]))
            own = bv[s, f] - (1.0 + 4.0 * k + react_s[f, f]) * out_u[s, f]
            if s == 0:
                res = res + first_step * own
            else:
                res = res + (own + out_u[0, f])
            out_res[s, f] = res

    pltpu.make_async_copy(pack.at[some], msgs.at[some], a_send).wait()
    pltpu.make_async_copy(m5.at[some], back5.at[some], r5_send).wait()
    pltpu.make_async_copy(m6.at[some], back6.at[some], r6_send).wait()

    @pl.when(last)
    def _():
        pltpu.make_async_copy(prev_s.at[some], prev_s.at[some], p_send).wait()

    @pl.loop(0, 5)
    def _(j):
        @pl.when(has_up)
        def _():
            row_copy(j, 0).wait_send()

        @pl.when(has_dn)
        def _():
            row_copy(j, 1).wait_send()

        col_copy(j, 0).wait_send()
        col_copy(j, 1).wait_send()

    @pl.when(jnp.logical_or(edge_up, edge_dn))
    def _():
        pltpu.make_async_copy(edge_s, edge_s, e_send).wait()


def shards(previous, right_side, kappa, drift, reaction):
    hbm = pl.BlockSpec(memory_space=pltpu.HBM)
    smem = pl.BlockSpec(memory_space=pltpu.SMEM)
    vmem = pl.BlockSpec(memory_space=pltpu.VMEM)
    shape = jax.ShapeDtypeStruct(right_side.shape, F32)
    dma = pltpu.SemaphoreType.DMA
    held = pltpu.VMEM((TM, 3, 8, 128), F32)
    folded = pltpu.VMEM((TM, 3, 4, 128), F32)
    natural = pltpu.VMEM((2, 3, 32, 512), F32)
    return pl.pallas_call(
        kernel,
        out_shape=(shape, shape),
        in_specs=[hbm, hbm, hbm, smem, smem],
        out_specs=(vmem, vmem),
        scratch_shapes=[
            natural,
            pltpu.VMEM((3, 32, 512), F32),
            pltpu.VMEM((3, 32, 512), F32),
            held, held, held,
            folded, pltpu.VMEM((3, 4, 128), F32),
            held, held, folded, held, folded, held,
            natural,
            pltpu.VMEM((5, 2, 3, 32, 128), F32),
            pltpu.VMEM((5, 2, 3, 32, 128), F32),
            pltpu.VMEM((5, 2, 3, 8, 128), F32),
            pltpu.VMEM((5, 2, 3, 8, 128), F32),
            pltpu.VMEM((TM, 4, 128), F32),
            pltpu.VMEM((2, 8, 4, 128), F32),
            pltpu.VMEM((2, 2, 4, 512), F32),
            pltpu.VMEM((11, 3, 8, 128), F32),
            pltpu.VMEM((2, 3, 32, 128), F32),
            pltpu.VMEM((2, 3, 8, 128), F32),
            dma((4,)),
            dma, dma, dma, dma,
            dma((5, 4)), dma((5, 4)),
            dma, dma, dma, dma,
            dma, dma((2,)), pltpu.SemaphoreType.REGULAR,
        ],
        compiler_params=pltpu.CompilerParams(
            collective_id=0, has_side_effects=True, vmem_limit_bytes=40 * 1024 * 1024),
    )(*[pltpu.with_memory_space_constraint(x, pltpu.HBM) for x in (right_side, previous, kappa, drift.T, reaction)])


def solution(mesh):
    in_specs = (
        P("tm", None, "space", None),
        P("tm", None, "space", None),
        P(None, "space", None),
        P(),
        P(),
    )
    out_specs = (P("tm", None, "space", None), P("tm", None, "space", None))
    return jax.shard_map(shards, mesh=mesh, in_specs=in_specs, out_specs=out_specs, check_vma=False)
```

```python
import functools

import jax
import jax.numpy as jnp
from jax import lax
from jax.experimental import pallas as pl
from jax.experimental.pallas import tpu as pltpu
from jax.sharding import PartitionSpec as P

ALPHA = 0.2
TM = 32
MESH = pl.DeviceIdType.MESH
F32 = jnp.float32


div, rem = lax.div, lax.rem


def place_of(r, c, odd):
    q = r + odd * (3 - 2 * r)
    half, y = div(c, 4), rem(c, 4)
    y = y + half * (3 - 2 * y)
    return y * 8 + q + half * (7 - 2 * q)


def tile_of(y, z, odd):
    half = div(z, 4)
    q = z + half * (7 - 2 * z)
    c = half * 4 + y + half * (3 - 2 * y)
    return (q + odd * (3 - 2 * q)) * 8 + c


HOPS = [(dy, dz) for dz in (4, 3, 5, 2, 6, 1, 7, 0) for dy in (2, 1, 3, 0) if (dy, dz) != (0, 0)]
UNROLL = 8


def kernel(
    b_hbm, prev_hbm, kappa_hbm, drift_s, react_s,
    out_u, out_res,
    bv, prev_v, kap, pack, msgs, held, prev_s, prev_r, ua, ub, m5, m6, back5, back6, wn,
    row_s, row_r, col_s, col_r, edge_s, edge_r, edge_n, coef, row_g, col_g,
    in_sem, a_send, a_recv, p_send, p_recv, h_send, h_recv, r5_send, r5_recv, r6_send, r6_recv, e_send, e_recv, ready,
):
    me = lax.axis_index("tm")
    sp = lax.axis_index("space")
    spaces = lax.axis_size("space")
    my, mz, odd_space = div(me, 8), rem(me, 8), rem(sp, 2)
    tile = tile_of(my, mz, odd_space)
    r, c = div(tile, 8), rem(tile, 8)
    places = [(rem(my + dy, 4), rem(mz + dz, 8)) for dy, dz in HOPS]
    peers = [y * 8 + z for y, z in places]

    load_b = pltpu.make_async_copy(b_hbm, bv, in_sem.at[0])
    load_k = pltpu.make_async_copy(kappa_hbm, kap, in_sem.at[1])
    load_p = pltpu.make_async_copy(prev_hbm.at[1], prev_v, in_sem.at[2])
    load_b.start()
    load_k.start()
    last = me == TM - 1

    @pl.when(last)
    def _():
        load_p.start()

    row_r[...] = jnp.zeros_like(row_r)
    edge_r[...] = jnp.zeros_like(edge_r)
    edge_s[...] = jnp.zeros_like(edge_s)

    barrier = pltpu.get_barrier_semaphore()
    for p in peers:
        pl.semaphore_signal(barrier, inc=1, device_id=(p, sp), device_id_type=MESH)

    @pl.when(sp > 0)
    def _():
        pl.semaphore_signal(barrier, inc=1, device_id=(me, sp - 1), device_id_type=MESH)

    @pl.when(sp < spaces - 1)
    def _():
        pl.semaphore_signal(barrier, inc=1, device_id=(me, sp + 1), device_id_type=MESH)

    edge_up = jnp.logical_and(r == 0, sp > 0)
    edge_dn = jnp.logical_and(r == 3, sp < spaces - 1)

    lane = lax.broadcasted_iota(jnp.int32, (8, 128), 1)
    sub = lax.broadcasted_iota(jnp.int32, (8, 128), 0)
    high = lane >= 64
    inner = lane % 64
    zero = jnp.zeros((8, 128), F32)

    def swap(x):
        return pltpu.roll(x, 64, 1)

    even_lane = rem(lane, 2) == 0
    first_odd = jnp.where(lane > 126, 0, lane) >= 63
    slot = jnp.where(even_lane, rem(lane, 64), rem(lane + 1, 64))

    def put_columns(m, x, packed):
        return jnp.where(slot == 2 * m, pltpu.roll(x, 2 * m, 1), packed)

    def fold_low(x):
        return jnp.where(high, pltpu.roll(swap(x), 4, 0), x)[0:4]

    def fold_high(x):
        return jnp.where(high, pltpu.roll(x, 4, 0), swap(x))[0:4]

    def unfold(x):
        return jnp.concatenate([x, swap(x)], axis=0)

    load_b.wait()

    @pl.loop(0, 4)
    def _(rr):
        rows = pl.ds(pl.multiple_of(rr * 8, 8), 8)
        for cp in range(4):
            cols = pl.ds(cp * 128, 128)
            for f in range(3):
                first = bv[0, f, rows, cols]
                second = bv[1, f, rows, cols]
                pack[rr * 8 + cp * 2, f] = jnp.where(high, swap(second), first)
                pack[rr * 8 + cp * 2 + 1, f] = jnp.where(high, second, swap(first))

    @pl.when(last)
    def _():
        load_p.wait()

        @pl.loop(0, 4)
        def _(rr):
            rows = pl.ds(pl.multiple_of(rr * 8, 8), 8)
            for cp in range(4):
                for f in range(3):
                    v = prev_v[f, rows, cp * 128:cp * 128 + 128]
                    prev_s[rr * 8 + cp * 2, f] = fold_low(v)
                    prev_s[rr * 8 + cp * 2 + 1, f] = fold_high(v)


    pl.semaphore_wait(barrier, TM - 1 + jnp.where(sp > 0, 1, 0) + jnp.where(sp < spaces - 1, 1, 0))

    @pl.when(last)
    def _():
        for p, (y, z) in zip(peers, places):
            pltpu.make_async_remote_copy(
                src_ref=prev_s.at[tile_of(y, z, odd_space)], dst_ref=prev_r, send_sem=p_send, recv_sem=p_recv,
                device_id=(p, sp), device_id_type=MESH).start()
        mine = pltpu.make_async_copy(prev_s.at[tile], prev_r, in_sem.at[2])
        mine.start()
        mine.wait()

    for p, (y, z) in zip(peers, places):
        pltpu.make_async_remote_copy(
            src_ref=pack.at[tile_of(y, z, odd_space)], dst_ref=msgs.at[me], send_sem=a_send, recv_sem=a_recv,
            device_id=(p, sp), device_id_type=MESH).start()
    own = pltpu.make_async_copy(pack.at[tile], msgs.at[me], in_sem.at[3])
    own.start()

    load_k.wait()
    rows = pl.ds(pl.multiple_of(r * 8, 8), 8)
    cols = pl.ds(pl.multiple_of(div(c, 2) * 128, 128), 128)
    upper_half = rem(c, 2) == 1
    keep = jnp.where(upper_half, lane, 127 - lane) >= 64
    ratio = []
    for f in range(3):
        k = kap[f, rows, cols]
        k = jnp.where(keep, k, swap(k))
        g = 1.0 / (1.0 + 4.0 * k + react_s[f, f])
        ratio.append(g)
        g2 = g * g
        g4 = g2 * g2
        g8 = g4 * g4
        g16 = g8 * g8
        g32 = g16 * g16
        below = g * (0.5 * drift_s[0, f] - k)
        above = g * (-0.5 * drift_s[0, f] - k)
        after = g * (0.5 * drift_s[1, f] - k)
        before = g * (-0.5 * drift_s[1, f] - k)
        d, e = [n for n in range(3) if n != f]
        coef[0, f] = jnp.where(sub == 7, 0.0, below)
        coef[1, f] = jnp.where(sub == 0, 0.0, above)
        coef[2, f] = jnp.where(inner == 63, 0.0, after)
        coef[3, f] = jnp.where(inner == 0, 0.0, before)
        coef[4, f] = g * react_s[f, d]
        coef[5, f] = g * react_s[f, e]
        coef[6, f] = jnp.where(sub == 7, below, jnp.where(sub == 0, above, 0.0))
        coef[7, f] = jnp.where(inner == 63, after, jnp.where(inner == 0, before, 0.0))
        coef[8, f] = g
        coef[9, f] = g32
        coef[10, f] = 1.0 / (1.0 - ALPHA * (g32 * g32))

    def power(i, carry):
        carry = list(carry)
        for u in range(UNROLL):
            m = i * UNROLL + u
            for f in range(3):
                w, packed = carry[2 * f:2 * f + 2]
                row_g[0, f, pl.ds(m, 1), :] = w[0:1]
                row_g[1, f, pl.ds(m, 1), :] = w[7:8]
                carry[2 * f:2 * f + 2] = [w * coef[8, f], put_columns(m, w, packed)]
        return tuple(carry)

    start = []
    for f in range(3):
        start += [ratio[f], zero]
    ends = lax.fori_loop(0, 32 // UNROLL, power, tuple(start))
    for f in range(3):
        col_g[f] = ends[2 * f + 1]

    left = place_of(r, rem(c + 7, 8), odd_space)
    right = place_of(r, rem(c + 1, 8), odd_space)
    up_in = r > 0
    dn_in = r < 3
    has_up = jnp.logical_or(up_in, sp > 0)
    has_dn = jnp.logical_or(dn_in, sp < spaces - 1)
    up_tm = jnp.where(up_in, place_of(jnp.maximum(r - 1, 0), c, odd_space), me)
    up_sp = jnp.where(up_in, sp, jnp.maximum(sp - 1, 0))
    dn_tm = jnp.where(dn_in, place_of(jnp.minimum(r + 1, 3), c, odd_space), me)
    dn_sp = jnp.where(dn_in, sp, jnp.minimum(sp + 1, spaces - 1))

    def row_copy(j, way):
        return pltpu.make_async_remote_copy(
            src_ref=row_s.at[j, way], dst_ref=row_r.at[j, way], send_sem=h_send.at[j, way], recv_sem=h_recv.at[j, way],
            device_id=((up_tm, up_sp), (dn_tm, dn_sp))[way], device_id_type=MESH)

    def col_copy(j, way):
        return pltpu.make_async_remote_copy(
            src_ref=col_s.at[j], dst_ref=col_r.at[j, way], send_sem=h_send.at[j, 2 + way],
            recv_sem=h_recv.at[j, 2 + way], device_id=((left, right)[way], sp), device_id_type=MESH)

    def carry_in(ends):
        out = []
        for f in range(3):
            end, other = ends[f], swap(ends[f])
            g32 = coef[9, f]
            final = (jnp.where(high, end, other) + g32 * jnp.where(high, other, end)) * coef[10, f]
            wrap = ALPHA * final
            out.append(jnp.where(high, other + g32 * wrap, wrap))
        return out

    def send_halo(j, came, columns):
        for f in range(3):
            x = came[f]
            ahead = jnp.where(even_lane, jnp.where(high, x[:, 64:65], x[:, 0:1]),
                              jnp.where(first_odd, x[:, 63:64], x[:, 127:128]))
            col_s[j, f] = columns[f] + col_g[f] * ahead
        col_copy(j, 0).start()
        col_copy(j, 1).start()
        for f in range(3):
            row_s[j, 0, f] = row_s[j, 0, f] + row_g[0, f] * came[f][0:1]
            row_s[j, 1, f] = row_s[j, 1, f] + row_g[1, f] * came[f][7:8]

        @pl.when(has_up)
        def _():
            row_copy(j, 0).start()

        @pl.when(has_dn)
        def _():
            row_copy(j, 1).start()

    def await_halo(j):
        @pl.when(has_dn)
        def _():
            row_copy(j, 0).wait_recv()

        @pl.when(has_up)
        def _():
            row_copy(j, 1).wait_recv()

        col_copy(j, 0).wait_recv()
        col_copy(j, 1).wait_recv()

    def pack_border(j, m, f, u, packed):
        row_s[j, 0, f, pl.ds(m, 1), :] = u[0:1]
        row_s[j, 1, f, pl.ds(m, 1), :] = u[7:8]
        return put_columns(m, u, packed)

    def interior(came, src, dst):
        def step(i, carry):
            carry = list(carry)
            for u in range(UNROLL):
                m = i * UNROLL + u
                v = []
                for f in range(3):
                    carry[f] = carry[f] * coef[8, f]
                    v.append(src[m, f] + carry[f])
                    if dst is not src:
                        src[m, f] = v[f]
                for f in range(3):
                    d, e = [n for n in range(3) if n != f]
                    off = (coef[0, f] * pltpu.roll(v[f], 7, 0) + coef[1, f] * pltpu.roll(v[f], 1, 0)
                           + coef[2, f] * pltpu.roll(v[f], 127, 1) + coef[3, f] * pltpu.roll(v[f], 1, 1)
                           + coef[4, f] * v[d] + coef[5, f] * v[e])
                    dst[m, f] = held[m, f] - off
            return tuple(carry)

        lax.fori_loop(0, 32 // UNROLL, step, tuple(came))

    def border_scan(j, dst, halo):
        ring = [jnp.where(even_lane, pltpu.roll(col_r[j, 1, f], 65, 1), pltpu.roll(col_r[j, 0, f], 63, 1))
                for f in range(3)]

        def step(i, carry):
            carry = list(carry)
            for u in range(UNROLL):
                m = i * UNROLL + u
                for f in range(3):
                    before, packed = carry[2 * f:2 * f + 2]
                    rows = jnp.where(sub == 0, row_r[j, 1, f, pl.ds(m, 1), :], row_r[j, 0, f, pl.ds(m, 1), :])
                    cols = pltpu.roll(ring[f], rem(128 - 2 * m, 128), 1)
                    x = dst[m, f] - (coef[6, f] * rows + coef[7, f] * cols)
                    now = x + coef[8, f] * before
                    dst[m, f] = now
                    if halo:
                        packed = pack_border(j + 1, m, f, now, packed)
                    carry[2 * f:2 * f + 2] = [now, packed]
            return tuple(carry)

        ends = lax.fori_loop(0, 32 // UNROLL, step, (zero,) * 6)
        return ends[0::2], ends[1::2]

    own.wait()
    some = pl.ds(0, TM - 1)
    pltpu.make_async_copy(pack.at[some], msgs.at[some], a_recv).wait()

    @pl.when(jnp.logical_not(last))
    def _():
        pltpu.make_async_copy(prev_r, prev_r, p_recv).wait()

    for f in range(3):
        p = unfold(prev_r[f])
        msgs[0, f] = msgs[0, f] - ALPHA * jnp.where(high, 0.0, p)

    def first(i, carry):
        carry = list(carry)
        for u in range(UNROLL // 2):
            h = i * (UNROLL // 2) + u
            for f in range(3):
                before, packed = carry[2 * f:2 * f + 2]
                g = coef[8, f]
                a, b = msgs[h, f], msgs[16 + h, f]
                even = g * jnp.where(high, swap(b), a)
                odd = g * jnp.where(high, b, swap(a))
                held[2 * h, f] = even
                held[2 * h + 1, f] = odd
                now = even + g * before
                ua[2 * h, f] = now
                packed = pack_border(0, 2 * h, f, now, packed)
                now = odd + g * now
                ua[2 * h + 1, f] = now
                packed = pack_border(0, 2 * h + 1, f, now, packed)
                carry[2 * f:2 * f + 2] = [now, packed]
        return tuple(carry)

    ends = lax.fori_loop(0, 32 // UNROLL, first, (zero,) * 6)
    came = carry_in(ends[0::2])
    send_halo(0, came, ends[1::2])

    @pl.when(sp > 0)
    def _():
        for n in range(8):
            pl.semaphore_signal(
                ready, inc=1, device_id=(place_of(3, jnp.int32(n), 1 - odd_space), sp - 1), device_id_type=MESH)

    @pl.when(sp < spaces - 1)
    def _():
        for n in range(8):
            pl.semaphore_signal(
                ready, inc=1, device_id=(place_of(0, jnp.int32(n), 1 - odd_space), sp + 1), device_id_type=MESH)

    def sweep(j, came):
        interior(came, ua, ua)
        await_halo(j)
        ends, columns = border_scan(j, ua, True)
        came = carry_in(ends)
        send_halo(j + 1, came, columns)
        return tuple(came)

    came = lax.fori_loop(0, 4, sweep, tuple(came))

    def fold_even(i, carry):
        for u in range(UNROLL // 2):
            h = i * (UNROLL // 2) + u
            for f in range(3):
                even = ua[2 * h, f]
                m5[h, f] = fold_low(even)
                m5[16 + h, f] = fold_high(even)
        return carry

    def to_messages(i, carry):
        carry = list(carry)
        for u in range(UNROLL // 2):
            h = i * (UNROLL // 2) + u
            for f in range(3):
                w = carry[f] * coef[8, f]
                even = ub[2 * h, f] + w
                w = w * coef[8, f]
                odd = ub[2 * h + 1, f] + w
                carry[f] = w
                fifth = ua[2 * h, f]
                one = jnp.where(high, swap(odd), even)
                two = jnp.where(high, odd, swap(even))
                m6[h, f] = one
                m6[16 + h, f] = two
                one = jnp.where(high, 0.0, fifth) * jnp.where(h == 0, 0.0, 1.0) - one
                two = jnp.where(high, 0.0, swap(fifth)) - two
                edge_s[h, f:f + 1, :] = jnp.where(r == 0, one[0:1], one[7:8])
                edge_s[16 + h, f:f + 1, :] = jnp.where(r == 0, two[0:1], two[7:8])
        return tuple(carry)

    def send_back(src, dst, send_sem, recv_sem, own_sem):
        for p in peers:
            pltpu.make_async_remote_copy(
                src_ref=src.at[p], dst_ref=dst.at[tile], send_sem=send_sem, recv_sem=recv_sem,
                device_id=(p, sp), device_id_type=MESH).start()
        own = pltpu.make_async_copy(src.at[me], dst.at[tile], own_sem)
        own.start()
        return own

    interior(came, ua, ub)
    lax.fori_loop(0, 32 // UNROLL, fold_even, 0)
    own5 = send_back(m5, back5, r5_send, r5_recv, in_sem.at[0])
    await_halo(4)
    ends, _ = border_scan(4, ub, False)
    lax.fori_loop(0, 32 // UNROLL, to_messages, tuple(carry_in(ends)))
    own6 = send_back(m6, back6, r6_send, r6_recv, in_sem.at[1])

    def send_edge(way):
        pl.semaphore_wait(ready, TM)
        for o in range(TM):
            p = rem(me + o, TM)
            pltpu.make_async_remote_copy(
                src_ref=edge_s.at[p], dst_ref=edge_r.at[way, c], send_sem=e_send, recv_sem=e_recv.at[way],
                device_id=(p, sp - 1 + 2 * way), device_id_type=MESH).start()

    @pl.when(edge_up)
    def _():
        send_edge(0)

    @pl.when(edge_dn)
    def _():
        send_edge(1)

    own5.wait()
    own6.wait()
    pltpu.make_async_copy(m5.at[some], back5.at[some], r5_recv).wait()
    pltpu.make_async_copy(m6.at[some], back6.at[some], r6_recv).wait()

    first_step = jnp.where(me == 0, 1.0, 0.0)

    @pl.loop(0, 4)
    def _(rr):
        rows = pl.ds(pl.multiple_of(rr * 8, 8), 8)
        for cp in range(4):
            cols = pl.ds(cp * 128, 128)
            t = rr * 8 + cp * 2
            for f in range(3):
                a6, b6 = back6[t, f], back6[t + 1, f]
                n0 = jnp.where(high, swap(b6), a6)
                n1 = jnp.where(high, b6, swap(a6))
                o0 = jnp.where(high, swap(unfold(back5[t + 1, f])), unfold(back5[t, f]))
                out_u[0, f, rows, cols] = n0
                out_u[1, f, rows, cols] = n1
                wn[0, f, rows, cols] = o0 * (1.0 - first_step) - n0
                wn[1, f, rows, cols] = -n1

    @pl.when(sp < spaces - 1)
    def _():
        pltpu.make_async_copy(edge_r.at[0], edge_r.at[0], e_recv.at[0]).wait()

    @pl.when(sp > 0)
    def _():
        pltpu.make_async_copy(edge_r.at[1], edge_r.at[1], e_recv.at[1]).wait()

    high4 = lax.broadcasted_iota(jnp.int32, (4, 128), 1) >= 64
    for way in range(2):
        for cp in range(4):
            a, b = edge_r[way, 2 * cp], edge_r[way, 2 * cp + 1]
            edge_n[way, 0, :, cp * 128:cp * 128 + 128] = jnp.where(high4, swap(b), a)
            edge_n[way, 1, :, cp * 128:cp * 128 + 128] = jnp.where(high4, b, swap(a))

    tall = lax.broadcasted_iota(jnp.int32, (32, 512), 0)
    for s in range(2):
        w = [wn[s, f] for f in range(3)]
        for f in range(3):
            k = kap[f]
            below = jnp.where(tall == 31, edge_n[0, s, f:f + 1, :], pltpu.roll(w[f], 31, 0))
            above = jnp.where(tall == 0, edge_n[1, s, f:f + 1, :], pltpu.roll(w[f], 1, 0))
            after = pltpu.roll(w[f], 511, 1)
            before = pltpu.roll(w[f], 1, 1)
            d, e = [n for n in range(3) if n != f]
            res = (0.5 * drift_s[0, f] * (below - above) + 0.5 * drift_s[1, f] * (after - before)
                   - k * (below + above + after + before) + (react_s[f, d] * w[d] + react_s[f, e] * w[e]))
            own = bv[s, f] - (1.0 + 4.0 * k + react_s[f, f]) * out_u[s, f]
            if s == 0:
                res = res + first_step * own
            else:
                res = res + (own + out_u[0, f])
            out_res[s, f] = res

    pltpu.make_async_copy(pack.at[some], msgs.at[some], a_send).wait()
    pltpu.make_async_copy(m5.at[some], back5.at[some], r5_send).wait()
    pltpu.make_async_copy(m6.at[some], back6.at[some], r6_send).wait()

    @pl.when(last)
    def _():
        pltpu.make_async_copy(prev_s.at[some], prev_s.at[some], p_send).wait()

    @pl.loop(0, 5)
    def _(j):
        @pl.when(has_up)
        def _():
            row_copy(j, 0).wait_send()

        @pl.when(has_dn)
        def _():
            row_copy(j, 1).wait_send()

        col_copy(j, 0).wait_send()
        col_copy(j, 1).wait_send()

    @pl.when(jnp.logical_or(edge_up, edge_dn))
    def _():
        pltpu.make_async_copy(edge_s, edge_s, e_send).wait()


def shards(previous, right_side, kappa, drift, reaction):
    hbm = pl.BlockSpec(memory_space=pltpu.HBM)
    smem = pl.BlockSpec(memory_space=pltpu.SMEM)
    vmem = pl.BlockSpec(memory_space=pltpu.VMEM)
    shape = jax.ShapeDtypeStruct(right_side.shape, F32)
    dma = pltpu.SemaphoreType.DMA
    held = pltpu.VMEM((TM, 3, 8, 128), F32)
    folded = pltpu.VMEM((TM, 3, 4, 128), F32)
    natural = pltpu.VMEM((2, 3, 32, 512), F32)
    return pl.pallas_call(
        kernel,
        out_shape=(shape, shape),
        in_specs=[hbm, hbm, hbm, smem, smem],
        out_specs=(vmem, vmem),
        scratch_shapes=[
            natural,
            pltpu.VMEM((3, 32, 512), F32),
            pltpu.VMEM((3, 32, 512), F32),
            held, held, held,
            folded, pltpu.VMEM((3, 4, 128), F32),
            held, held, folded, held, folded, held,
            natural,
            pltpu.VMEM((5, 2, 3, 32, 128), F32),
            pltpu.VMEM((5, 2, 3, 32, 128), F32),
            pltpu.VMEM((5, 3, 8, 128), F32),
            pltpu.VMEM((5, 2, 3, 8, 128), F32),
            pltpu.VMEM((TM, 4, 128), F32),
            pltpu.VMEM((2, 8, 4, 128), F32),
            pltpu.VMEM((2, 2, 4, 512), F32),
            pltpu.VMEM((11, 3, 8, 128), F32),
            pltpu.VMEM((2, 3, 32, 128), F32),
            pltpu.VMEM((3, 8, 128), F32),
            dma((4,)),
            dma, dma, dma, dma,
            dma((5, 4)), dma((5, 4)),
            dma, dma, dma, dma,
            dma, dma((2,)), pltpu.SemaphoreType.REGULAR,
        ],
        compiler_params=pltpu.CompilerParams(
            collective_id=0, has_side_effects=True, vmem_limit_bytes=40 * 1024 * 1024),
    )(*[pltpu.with_memory_space_constraint(x, pltpu.HBM) for x in (right_side, previous, kappa, drift.T, reaction)])


def solution(mesh):
    in_specs = (
        P("tm", None, "space", None),
        P("tm", None, "space", None),
        P(None, "space", None),
        P(),
        P(),
    )
    out_specs = (P("tm", None, "space", None), P("tm", None, "space", None))
    return jax.shard_map(shards, mesh=mesh, in_specs=in_specs, out_specs=out_specs, check_vma=False)
```

```python
import functools

import jax
import jax.numpy as jnp
from jax import lax
from jax.experimental import pallas as pl
from jax.experimental.pallas import tpu as pltpu
from jax.sharding import PartitionSpec as P

ALPHA = 0.2
TM = 32
MESH = pl.DeviceIdType.MESH
F32 = jnp.float32


div, rem = lax.div, lax.rem


def place_of(r, c, odd):
    q = r + odd * (3 - 2 * r)
    half, y = div(c, 4), rem(c, 4)
    y = y + half * (3 - 2 * y)
    return y * 8 + q + half * (7 - 2 * q)


def tile_of(y, z, odd):
    half = div(z, 4)
    q = z + half * (7 - 2 * z)
    c = half * 4 + y + half * (3 - 2 * y)
    return (q + odd * (3 - 2 * q)) * 8 + c


HOPS = [(dy, dz) for dz in (4, 3, 5, 2, 6, 1, 7, 0) for dy in (2, 1, 3, 0) if (dy, dz) != (0, 0)]
UNROLL = 8


def kernel(
    b_hbm, prev_hbm, kappa_hbm, drift_s, react_s,
    out_u, out_res,
    bv, prev_v, kap, pack, msgs, held, prev_s, prev_r, ua, ub, m5, m6, back5, back6, wn,
    row_s, row_r, col_s, col_r, edge_s, edge_r, edge_n, coef, row_g, col_g,
    in_sem, a_send, a_recv, p_send, p_recv, h_send, h_recv, r5_send, r5_recv, r6_send, r6_recv, e_send, e_recv, ready,
):
    me = lax.axis_index("tm")
    sp = lax.axis_index("space")
    spaces = lax.axis_size("space")
    my, mz, odd_space = div(me, 8), rem(me, 8), rem(sp, 2)
    tile = tile_of(my, mz, odd_space)
    r, c = div(tile, 8), rem(tile, 8)
    places = [(rem(my + dy, 4), rem(mz + dz, 8)) for dy, dz in HOPS]
    peers = [y * 8 + z for y, z in places]

    load_b = pltpu.make_async_copy(b_hbm, bv, in_sem.at[0])
    load_k = pltpu.make_async_copy(kappa_hbm, kap, in_sem.at[1])
    load_p = pltpu.make_async_copy(prev_hbm.at[1], prev_v, in_sem.at[2])
    load_b.start()
    load_k.start()
    last = me == TM - 1

    @pl.when(last)
    def _():
        load_p.start()

    row_r[...] = jnp.zeros_like(row_r)
    edge_r[...] = jnp.zeros_like(edge_r)
    edge_s[...] = jnp.zeros_like(edge_s)

    barrier = pltpu.get_barrier_semaphore()
    for p in peers:
        pl.semaphore_signal(barrier, inc=1, device_id=(p, sp), device_id_type=MESH)

    @pl.when(sp > 0)
    def _():
        pl.semaphore_signal(barrier, inc=1, device_id=(me, sp - 1), device_id_type=MESH)

    @pl.when(sp < spaces - 1)
    def _():
        pl.semaphore_signal(barrier, inc=1, device_id=(me, sp + 1), device_id_type=MESH)

    edge_up = jnp.logical_and(r == 0, sp > 0)
    edge_dn = jnp.logical_and(r == 3, sp < spaces - 1)

    lane = lax.broadcasted_iota(jnp.int32, (8, 128), 1)
    sub = lax.broadcasted_iota(jnp.int32, (8, 128), 0)
    high = lane >= 64
    inner = lane % 64
    zero = jnp.zeros((8, 128), F32)

    def swap(x):
        return pltpu.roll(x, 64, 1)

    even_lane = rem(lane, 2) == 0
    first_odd = jnp.where(lane > 126, 0, lane) >= 63
    slot = jnp.where(even_lane, rem(lane, 64), rem(lane + 1, 64))

    def put_columns(m, x, packed):
        return jnp.where(slot == 2 * m, pltpu.roll(x, 2 * m, 1), packed)

    def fold_low(x):
        return jnp.where(high, pltpu.roll(swap(x), 4, 0), x)[0:4]

    def fold_high(x):
        return jnp.where(high, pltpu.roll(x, 4, 0), swap(x))[0:4]

    def unfold(x):
        return jnp.concatenate([x, swap(x)], axis=0)

    load_b.wait()

    @pl.loop(0, 4)
    def _(rr):
        rows = pl.ds(pl.multiple_of(rr * 8, 8), 8)
        for cp in range(4):
            cols = pl.ds(cp * 128, 128)
            for f in range(3):
                first = bv[0, f, rows, cols]
                second = bv[1, f, rows, cols]
                pack[rr * 8 + cp * 2, f] = jnp.where(high, swap(second), first)
                pack[rr * 8 + cp * 2 + 1, f] = jnp.where(high, second, swap(first))

    @pl.when(last)
    def _():
        load_p.wait()

        @pl.loop(0, 4)
        def _(rr):
            rows = pl.ds(pl.multiple_of(rr * 8, 8), 8)
            for cp in range(4):
                for f in range(3):
                    v = prev_v[f, rows, cp * 128:cp * 128 + 128]
                    prev_s[rr * 8 + cp * 2, f] = fold_low(v)
                    prev_s[rr * 8 + cp * 2 + 1, f] = fold_high(v)


    pl.semaphore_wait(barrier, TM - 1 + jnp.where(sp > 0, 1, 0) + jnp.where(sp < spaces - 1, 1, 0))

    @pl.when(last)
    def _():
        for p, (y, z) in zip(peers, places):
            pltpu.make_async_remote_copy(
                src_ref=prev_s.at[tile_of(y, z, odd_space)], dst_ref=prev_r, send_sem=p_send, recv_sem=p_recv,
                device_id=(p, sp), device_id_type=MESH).start()
        mine = pltpu.make_async_copy(prev_s.at[tile], prev_r, in_sem.at[2])
        mine.start()
        mine.wait()

    for p, (y, z) in zip(peers, places):
        pltpu.make_async_remote_copy(
            src_ref=pack.at[tile_of(y, z, odd_space)], dst_ref=msgs.at[me], send_sem=a_send, recv_sem=a_recv,
            device_id=(p, sp), device_id_type=MESH).start()
    own = pltpu.make_async_copy(pack.at[tile], msgs.at[me], in_sem.at[3])
    own.start()

    load_k.wait()
    rows = pl.ds(pl.multiple_of(r * 8, 8), 8)
    cols = pl.ds(pl.multiple_of(div(c, 2) * 128, 128), 128)
    upper_half = rem(c, 2) == 1
    keep = jnp.where(upper_half, lane, 127 - lane) >= 64
    ratio = []
    for f in range(3):
        k = kap[f, rows, cols]
        k = jnp.where(keep, k, swap(k))
        g = 1.0 / (1.0 + 4.0 * k + react_s[f, f])
        ratio.append(g)
        g2 = g * g
        g4 = g2 * g2
        g8 = g4 * g4
        g16 = g8 * g8
        g32 = g16 * g16
        below = g * (0.5 * drift_s[0, f] - k)
        above = g * (-0.5 * drift_s[0, f] - k)
        after = g * (0.5 * drift_s[1, f] - k)
        before = g * (-0.5 * drift_s[1, f] - k)
        d, e = [n for n in range(3) if n != f]
        coef[0, f] = jnp.where(sub == 7, 0.0, below)
        coef[1, f] = jnp.where(sub == 0, 0.0, above)
        coef[2, f] = jnp.where(inner == 63, 0.0, after)
        coef[3, f] = jnp.where(inner == 0, 0.0, before)
        coef[4, f] = g * react_s[f, d]
        coef[5, f] = g * react_s[f, e]
        coef[6, f] = jnp.where(sub == 7, below, jnp.where(sub == 0, above, 0.0))
        coef[7, f] = jnp.where(inner == 63, after, jnp.where(inner == 0, before, 0.0))
        coef[8, f] = g
        coef[9, f] = g32
        coef[10, f] = 1.0 / (1.0 - ALPHA * (g32 * g32))

    def power(i, carry):
        carry = list(carry)
        for u in range(UNROLL):
            m = i * UNROLL + u
            for f in range(3):
                w, packed = carry[2 * f:2 * f + 2]
                row_g[0, f, pl.ds(m, 1), :] = w[0:1]
                row_g[1, f, pl.ds(m, 1), :] = w[7:8]
                carry[2 * f:2 * f + 2] = [w * coef[8, f], put_columns(m, w, packed)]
        return tuple(carry)

    start = []
    for f in range(3):
        start += [ratio[f], zero]
    ends = lax.fori_loop(0, 32 // UNROLL, power, tuple(start))
    for f in range(3):
        col_g[f] = ends[2 * f + 1]

    left = place_of(r, rem(c + 7, 8), odd_space)
    right = place_of(r, rem(c + 1, 8), odd_space)
    up_in = r > 0
    dn_in = r < 3
    has_up = jnp.logical_or(up_in, sp > 0)
    has_dn = jnp.logical_or(dn_in, sp < spaces - 1)
    up_tm = jnp.where(up_in, place_of(jnp.maximum(r - 1, 0), c, odd_space), me)
    up_sp = jnp.where(up_in, sp, jnp.maximum(sp - 1, 0))
    dn_tm = jnp.where(dn_in, place_of(jnp.minimum(r + 1, 3), c, odd_space), me)
    dn_sp = jnp.where(dn_in, sp, jnp.minimum(sp + 1, spaces - 1))

    def row_copy(j, way):
        return pltpu.make_async_remote_copy(
            src_ref=row_s.at[j, way], dst_ref=row_r.at[j, way], send_sem=h_send.at[j, way], recv_sem=h_recv.at[j, way],
            device_id=((up_tm, up_sp), (dn_tm, dn_sp))[way], device_id_type=MESH)

    def col_copy(j, way):
        return pltpu.make_async_remote_copy(
            src_ref=col_s.at[j], dst_ref=col_r.at[j, way], send_sem=h_send.at[j, 2 + way],
            recv_sem=h_recv.at[j, 2 + way], device_id=((left, right)[way], sp), device_id_type=MESH)

    def carry_in(ends):
        out = []
        for f in range(3):
            end, other = ends[f], swap(ends[f])
            g32 = coef[9, f]
            final = (jnp.where(high, end, other) + g32 * jnp.where(high, other, end)) * coef[10, f]
            wrap = ALPHA * final
            out.append(jnp.where(high, other + g32 * wrap, wrap))
        return out

    def send_halo(j, came, columns):
        for f in range(3):
            x = came[f]
            ahead = jnp.where(even_lane, jnp.where(high, x[:, 64:65], x[:, 0:1]),
                              jnp.where(first_odd, x[:, 63:64], x[:, 127:128]))
            col_s[j, f] = columns[f] + col_g[f] * ahead
        col_copy(j, 0).start()
        col_copy(j, 1).start()
        for f in range(3):
            row_s[j, 0, f] = row_s[j, 0, f] + row_g[0, f] * came[f][0:1]
            row_s[j, 1, f] = row_s[j, 1, f] + row_g[1, f] * came[f][7:8]

        @pl.when(has_up)
        def _():
            row_copy(j, 0).start()

        @pl.when(has_dn)
        def _():
            row_copy(j, 1).start()

    def await_halo(j):
        @pl.when(has_dn)
        def _():
            row_copy(j, 0).wait_recv()

        @pl.when(has_up)
        def _():
            row_copy(j, 1).wait_recv()

        col_copy(j, 0).wait_recv()
        col_copy(j, 1).wait_recv()

    def pack_border(j, m, f, u, packed):
        row_s[j, 0, f, pl.ds(m, 1), :] = u[0:1]
        row_s[j, 1, f, pl.ds(m, 1), :] = u[7:8]
        return put_columns(m, u, packed)

    def interior(came, src, dst):
        def step(i, carry):
            carry = list(carry)
            for u in range(UNROLL):
                m = i * UNROLL + u
                v = []
                for f in range(3):
                    carry[f] = carry[f] * coef[8, f]
                    v.append(src[m, f] + carry[f])
                    if dst is not src:
                        src[m, f] = v[f]
                for f in range(3):
                    d, e = [n for n in range(3) if n != f]
                    off = (coef[0, f] * pltpu.roll(v[f], 7, 0) + coef[1, f] * pltpu.roll(v[f], 1, 0)
                           + coef[2, f] * pltpu.roll(v[f], 127, 1) + coef[3, f] * pltpu.roll(v[f], 1, 1)
                           + coef[4, f] * v[d] + coef[5, f] * v[e])
                    dst[m, f] = held[m, f] - off
            return tuple(carry)

        lax.fori_loop(0, 32 // UNROLL, step, tuple(came))

    def border_scan(j, dst, halo):
        ring = [jnp.where(even_lane, pltpu.roll(col_r[j, 1, f], 65, 1), pltpu.roll(col_r[j, 0, f], 63, 1))
                for f in range(3)]

        def step(i, carry):
            carry = list(carry)
            for u in range(UNROLL):
                m = i * UNROLL + u
                for f in range(3):
                    before, packed = carry[2 * f:2 * f + 2]
                    rows = jnp.where(sub == 0, row_r[j, 1, f, pl.ds(m, 1), :], row_r[j, 0, f, pl.ds(m, 1), :])
                    cols = pltpu.roll(ring[f], rem(128 - 2 * m, 128), 1)
                    x = dst[m, f] - (coef[6, f] * rows + coef[7, f] * cols)
                    now = x + coef[8, f] * before
                    dst[m, f] = now
                    if halo:
                        packed = pack_border(j + 1, m, f, now, packed)
                    carry[2 * f:2 * f + 2] = [now, packed]
            return tuple(carry)

        ends = lax.fori_loop(0, 32 // UNROLL, step, (zero,) * 6)
        return ends[0::2], ends[1::2]

    own.wait()
    some = pl.ds(0, TM - 1)
    pltpu.make_async_copy(pack.at[some], msgs.at[some], a_recv).wait()

    @pl.when(jnp.logical_not(last))
    def _():
        pltpu.make_async_copy(prev_r, prev_r, p_recv).wait()

    for f in range(3):
        p = unfold(prev_r[f])
        msgs[0, f] = msgs[0, f] - ALPHA * jnp.where(high, 0.0, p)

    def first(i, carry):
        carry = list(carry)
        for u in range(UNROLL // 2):
            h = i * (UNROLL // 2) + u
            for f in range(3):
                before, packed = carry[2 * f:2 * f + 2]
                g = coef[8, f]
                a, b = msgs[h, f], msgs[16 + h, f]
                even = g * jnp.where(high, swap(b), a)
                odd = g * jnp.where(high, b, swap(a))
                held[2 * h, f] = even
                held[2 * h + 1, f] = odd
                now = even + g * before
                ua[2 * h, f] = now
                packed = pack_border(0, 2 * h, f, now, packed)
                now = odd + g * now
                ua[2 * h + 1, f] = now
                packed = pack_border(0, 2 * h + 1, f, now, packed)
                carry[2 * f:2 * f + 2] = [now, packed]
        return tuple(carry)

    ends = lax.fori_loop(0, 32 // UNROLL, first, (zero,) * 6)
    came = carry_in(ends[0::2])
    send_halo(0, came, ends[1::2])

    @pl.when(sp > 0)
    def _():
        for n in range(8):
            pl.semaphore_signal(
                ready, inc=1, device_id=(place_of(3, jnp.int32(n), 1 - odd_space), sp - 1), device_id_type=MESH)

    @pl.when(sp < spaces - 1)
    def _():
        for n in range(8):
            pl.semaphore_signal(
                ready, inc=1, device_id=(place_of(0, jnp.int32(n), 1 - odd_space), sp + 1), device_id_type=MESH)

    def sweep(j, came):
        interior(came, ua, ua)
        await_halo(j)
        ends, columns = border_scan(j, ua, True)
        came = carry_in(ends)
        send_halo(j + 1, came, columns)
        return tuple(came)

    came = lax.fori_loop(0, 4, sweep, tuple(came))

    def fold_even(i, carry):
        for u in range(UNROLL // 2):
            h = i * (UNROLL // 2) + u
            for f in range(3):
                even = ua[2 * h, f]
                m5[h, f] = fold_low(even)
                m5[16 + h, f] = fold_high(even)
        return carry

    def to_messages(i, carry):
        carry = list(carry)
        for u in range(UNROLL // 2):
            h = i * (UNROLL // 2) + u
            for f in range(3):
                w = carry[f] * coef[8, f]
                even = ub[2 * h, f] + w
                w = w * coef[8, f]
                odd = ub[2 * h + 1, f] + w
                carry[f] = w
                fifth = ua[2 * h, f]
                one = jnp.where(high, swap(odd), even)
                two = jnp.where(high, odd, swap(even))
                m6[h, f] = one
                m6[16 + h, f] = two
                one = jnp.where(high, 0.0, fifth) * jnp.where(h == 0, 0.0, 1.0) - one
                two = jnp.where(high, 0.0, swap(fifth)) - two
                edge_s[h, f:f + 1, :] = jnp.where(r == 0, one[0:1], one[7:8])
                edge_s[16 + h, f:f + 1, :] = jnp.where(r == 0, two[0:1], two[7:8])
        return tuple(carry)

    def send_back(src, dst, send_sem, recv_sem, own_sem):
        for p in peers:
            pltpu.make_async_remote_copy(
                src_ref=src.at[p], dst_ref=dst.at[tile], send_sem=send_sem, recv_sem=recv_sem,
                device_id=(p, sp), device_id_type=MESH).start()
        own = pltpu.make_async_copy(src.at[me], dst.at[tile], own_sem)
        own.start()
        return own

    interior(came, ua, ub)
    lax.fori_loop(0, 32 // UNROLL, fold_even, 0)
    own5 = send_back(m5, back5, r5_send, r5_recv, in_sem.at[0])
    await_halo(4)
    ends, _ = border_scan(4, ub, False)
    lax.fori_loop(0, 32 // UNROLL, to_messages, tuple(carry_in(ends)))
    own6 = send_back(m6, back6, r6_send, r6_recv, in_sem.at[1])

    def send_edge(way):
        pl.semaphore_wait(ready, TM)
        for o in range(TM):
            p = rem(me + o, TM)
            pltpu.make_async_remote_copy(
                src_ref=edge_s.at[p], dst_ref=edge_r.at[way, c], send_sem=e_send, recv_sem=e_recv.at[way],
                device_id=(p, sp - 1 + 2 * way), device_id_type=MESH).start()

    @pl.when(edge_up)
    def _():
        send_edge(0)

    @pl.when(edge_dn)
    def _():
        send_edge(1)

    own5.wait()
    own6.wait()
    pltpu.make_async_copy(m5.at[some], back5.at[some], r5_recv).wait()
    pltpu.make_async_copy(m6.at[some], back6.at[some], r6_recv).wait()

    first_step = jnp.where(me == 0, 1.0, 0.0)

    @pl.loop(0, 4)
    def _(rr):
        rows = pl.ds(pl.multiple_of(rr * 8, 8), 8)
        for cp in range(4):
            cols = pl.ds(cp * 128, 128)
            t = rr * 8 + cp * 2
            for f in range(3):
                a6, b6 = back6[t, f], back6[t + 1, f]
                n0 = jnp.where(high, swap(b6), a6)
                n1 = jnp.where(high, b6, swap(a6))
                o0 = jnp.where(high, swap(unfold(back5[t + 1, f])), unfold(back5[t, f]))
                out_u[0, f, rows, cols] = n0
                out_u[1, f, rows, cols] = n1
                wn[0, f, rows, cols] = o0 * (1.0 - first_step) - n0
                wn[1, f, rows, cols] = -n1

    @pl.when(sp < spaces - 1)
    def _():
        pltpu.make_async_copy(edge_r.at[0], edge_r.at[0], e_recv.at[0]).wait()

    @pl.when(sp > 0)
    def _():
        pltpu.make_async_copy(edge_r.at[1], edge_r.at[1], e_recv.at[1]).wait()

    high4 = lax.broadcasted_iota(jnp.int32, (4, 128), 1) >= 64
    for way in range(2):
        for cp in range(4):
            a, b = edge_r[way, 2 * cp], edge_r[way, 2 * cp + 1]
            edge_n[way, 0, :, cp * 128:cp * 128 + 128] = jnp.where(high4, swap(b), a)
            edge_n[way, 1, :, cp * 128:cp * 128 + 128] = jnp.where(high4, b, swap(a))

    tall = lax.broadcasted_iota(jnp.int32, (32, 512), 0)
    for s in range(2):
        w = [wn[s, f] for f in range(3)]
        for f in range(3):
            k = kap[f]
            below = jnp.where(tall == 31, edge_n[0, s, f:f + 1, :], pltpu.roll(w[f], 31, 0))
            above = jnp.where(tall == 0, edge_n[1, s, f:f + 1, :], pltpu.roll(w[f], 1, 0))
            after = pltpu.roll(w[f], 511, 1)
            before = pltpu.roll(w[f], 1, 1)
            d, e = [n for n in range(3) if n != f]
            res = (0.5 * drift_s[0, f] * (below - above) + 0.5 * drift_s[1, f] * (after - before)
                   - k * (below + above + after + before) + (react_s[f, d] * w[d] + react_s[f, e] * w[e]))
            own = bv[s, f] - (1.0 + 4.0 * k + react_s[f, f]) * out_u[s, f]
            if s == 0:
                res = res + first_step * own
            else:
                res = res + (own + out_u[0, f])
            out_res[s, f] = res

    pltpu.make_async_copy(pack.at[some], msgs.at[some], a_send).wait()
    pltpu.make_async_copy(m5.at[some], back5.at[some], r5_send).wait()
    pltpu.make_async_copy(m6.at[some], back6.at[some], r6_send).wait()

    @pl.when(last)
    def _():
        pltpu.make_async_copy(prev_s.at[some], prev_s.at[some], p_send).wait()

    @pl.loop(0, 5)
    def _(j):
        @pl.when(has_up)
        def _():
            row_copy(j, 0).wait_send()

        @pl.when(has_dn)
        def _():
            row_copy(j, 1).wait_send()

        col_copy(j, 0).wait_send()
        col_copy(j, 1).wait_send()

    @pl.when(jnp.logical_or(edge_up, edge_dn))
    def _():
        pltpu.make_async_copy(edge_s, edge_s, e_send).wait()


def write_out(u, res, out_u, out_res, sem):
    copies = [pltpu.make_async_copy(u, out_u, sem.at[0]), pltpu.make_async_copy(res, out_res, sem.at[1])]
    for copy in copies:
        copy.start()
    for copy in copies:
        copy.wait()


def shards(previous, right_side, kappa, drift, reaction):
    hbm = pl.BlockSpec(memory_space=pltpu.HBM)
    smem = pl.BlockSpec(memory_space=pltpu.SMEM)
    vmem = pl.BlockSpec(memory_space=pltpu.VMEM)
    shape = jax.ShapeDtypeStruct(right_side.shape, F32)
    dma = pltpu.SemaphoreType.DMA
    held = pltpu.VMEM((TM, 3, 8, 128), F32)
    folded = pltpu.VMEM((TM, 3, 4, 128), F32)
    natural = pltpu.VMEM((2, 3, 32, 512), F32)
    results = pl.pallas_call(
        kernel,
        out_shape=(shape, shape),
        in_specs=[hbm, hbm, hbm, smem, smem],
        out_specs=(vmem, vmem),
        scratch_shapes=[
            natural,
            pltpu.VMEM((3, 32, 512), F32),
            pltpu.VMEM((3, 32, 512), F32),
            held, held, held,
            folded, pltpu.VMEM((3, 4, 128), F32),
            held, held, folded, held, folded, held,
            natural,
            pltpu.VMEM((5, 2, 3, 32, 128), F32),
            pltpu.VMEM((5, 2, 3, 32, 128), F32),
            pltpu.VMEM((5, 3, 8, 128), F32),
            pltpu.VMEM((5, 2, 3, 8, 128), F32),
            pltpu.VMEM((TM, 4, 128), F32),
            pltpu.VMEM((2, 8, 4, 128), F32),
            pltpu.VMEM((2, 2, 4, 512), F32),
            pltpu.VMEM((11, 3, 8, 128), F32),
            pltpu.VMEM((2, 3, 32, 128), F32),
            pltpu.VMEM((3, 8, 128), F32),
            dma((4,)),
            dma, dma, dma, dma,
            dma((5, 4)), dma((5, 4)),
            dma, dma, dma, dma,
            dma, dma((2,)), pltpu.SemaphoreType.REGULAR,
        ],
        compiler_params=pltpu.CompilerParams(
            collective_id=0, has_side_effects=True, vmem_limit_bytes=40 * 1024 * 1024),
    )(*[pltpu.with_memory_space_constraint(x, pltpu.HBM) for x in (right_side, previous, kappa, drift.T, reaction)])
    return pl.pallas_call(
        write_out,
        out_shape=(shape, shape),
        in_specs=[vmem, vmem],
        out_specs=(hbm, hbm),
        scratch_shapes=[dma((2,))],
    )(*[pltpu.with_memory_space_constraint(x, pltpu.VMEM) for x in results])


def solution(mesh):
    in_specs = (
        P("tm", None, "space", None),
        P("tm", None, "space", None),
        P(None, "space", None),
        P(),
        P(),
    )
    out_specs = (P("tm", None, "space", None), P("tm", None, "space", None))
    return jax.shard_map(shards, mesh=mesh, in_specs=in_specs, out_specs=out_specs, check_vma=False)
```

```python
import functools

import jax
import jax.numpy as jnp
from jax import lax
from jax.experimental import pallas as pl
from jax.experimental.pallas import tpu as pltpu
from jax.sharding import PartitionSpec as P

ALPHA = 0.2
TM = 32
MESH = pl.DeviceIdType.MESH
F32 = jnp.float32


div, rem = lax.div, lax.rem


def place_of(r, c, odd):
    q = r + odd * (3 - 2 * r)
    half, y = div(c, 4), rem(c, 4)
    y = y + half * (3 - 2 * y)
    return y * 8 + q + half * (7 - 2 * q)


def tile_of(y, z, odd):
    half = div(z, 4)
    q = z + half * (7 - 2 * z)
    c = half * 4 + y + half * (3 - 2 * y)
    return (q + odd * (3 - 2 * q)) * 8 + c


HOPS = [(dy, dz) for dz in (4, 3, 5, 2, 6, 1, 7, 0) for dy in (2, 1, 3, 0) if (dy, dz) != (0, 0)]
UNROLL = 8


def kernel(
    b_hbm, prev_hbm, kappa_hbm, drift_s, react_s,
    out_u, out_res,
    bv, prev_v, kap, pack, msgs, held, prev_s, prev_r, ua, ub, m5, m6, back5, back6, wn,
    row_s, row_r, col_s, col_r, edge_s, edge_r, edge_n, coef, row_g, col_g,
    in_sem, a_send, a_recv, p_send, p_recv, h_send, h_recv, r5_send, r5_recv, r6_send, r6_recv, e_send, e_recv, ready,
):
    me = lax.axis_index("tm")
    sp = lax.axis_index("space")
    spaces = lax.axis_size("space")
    my, mz, odd_space = div(me, 8), rem(me, 8), rem(sp, 2)
    tile = tile_of(my, mz, odd_space)
    r, c = div(tile, 8), rem(tile, 8)
    places = [(rem(my + dy, 4), rem(mz + dz, 8)) for dy, dz in HOPS]
    peers = [y * 8 + z for y, z in places]

    load_b = pltpu.make_async_copy(b_hbm, bv, in_sem.at[0])
    load_k = pltpu.make_async_copy(kappa_hbm, kap, in_sem.at[1])
    load_p = pltpu.make_async_copy(prev_hbm.at[1], prev_v, in_sem.at[2])
    load_b.start()
    load_k.start()
    last = me == TM - 1

    @pl.when(last)
    def _():
        load_p.start()

    row_r[...] = jnp.zeros_like(row_r)
    edge_r[...] = jnp.zeros_like(edge_r)
    edge_s[...] = jnp.zeros_like(edge_s)

    barrier = pltpu.get_barrier_semaphore()
    for p in peers:
        pl.semaphore_signal(barrier, inc=1, device_id=(p, sp), device_id_type=MESH)

    @pl.when(sp > 0)
    def _():
        pl.semaphore_signal(barrier, inc=1, device_id=(me, sp - 1), device_id_type=MESH)

    @pl.when(sp < spaces - 1)
    def _():
        pl.semaphore_signal(barrier, inc=1, device_id=(me, sp + 1), device_id_type=MESH)

    edge_up = jnp.logical_and(r == 0, sp > 0)
    edge_dn = jnp.logical_and(r == 3, sp < spaces - 1)

    lane = lax.broadcasted_iota(jnp.int32, (8, 128), 1)
    sub = lax.broadcasted_iota(jnp.int32, (8, 128), 0)
    high = lane >= 64
    inner = lane % 64
    zero = jnp.zeros((8, 128), F32)

    def swap(x):
        return pltpu.roll(x, 64, 1)

    even_lane = rem(lane, 2) == 0
    first_odd = jnp.where(lane > 126, 0, lane) >= 63
    slot = jnp.where(even_lane, rem(lane, 64), rem(lane + 1, 64))

    def put_columns(m, x, packed):
        return jnp.where(slot == 2 * m, pltpu.roll(x, 2 * m, 1), packed)

    def fold_low(x):
        return jnp.where(high, pltpu.roll(swap(x), 4, 0), x)[0:4]

    def fold_high(x):
        return jnp.where(high, pltpu.roll(x, 4, 0), swap(x))[0:4]

    def unfold(x):
        return jnp.concatenate([x, swap(x)], axis=0)

    load_b.wait()

    @pl.loop(0, 4)
    def _(rr):
        rows = pl.ds(pl.multiple_of(rr * 8, 8), 8)
        for cp in range(4):
            cols = pl.ds(cp * 128, 128)
            for f in range(3):
                first = bv[0, f, rows, cols]
                second = bv[1, f, rows, cols]
                pack[rr * 8 + cp * 2, f] = jnp.where(high, swap(second), first)
                pack[rr * 8 + cp * 2 + 1, f] = jnp.where(high, second, swap(first))

    @pl.when(last)
    def _():
        load_p.wait()

        @pl.loop(0, 4)
        def _(rr):
            rows = pl.ds(pl.multiple_of(rr * 8, 8), 8)
            for cp in range(4):
                for f in range(3):
                    v = prev_v[f, rows, cp * 128:cp * 128 + 128]
                    prev_s[rr * 8 + cp * 2, f] = fold_low(v)
                    prev_s[rr * 8 + cp * 2 + 1, f] = fold_high(v)


    pl.semaphore_wait(barrier, TM - 1 + jnp.where(sp > 0, 1, 0) + jnp.where(sp < spaces - 1, 1, 0))

    @pl.when(last)
    def _():
        for p, (y, z) in zip(peers, places):
            pltpu.make_async_remote_copy(
                src_ref=prev_s.at[tile_of(y, z, odd_space)], dst_ref=prev_r, send_sem=p_send, recv_sem=p_recv,
                device_id=(p, sp), device_id_type=MESH).start()
        mine = pltpu.make_async_copy(prev_s.at[tile], prev_r, in_sem.at[2])
        mine.start()
        mine.wait()

    for p, (y, z) in zip(peers, places):
        pltpu.make_async_remote_copy(
            src_ref=pack.at[tile_of(y, z, odd_space)], dst_ref=msgs.at[me], send_sem=a_send, recv_sem=a_recv,
            device_id=(p, sp), device_id_type=MESH).start()
    own = pltpu.make_async_copy(pack.at[tile], msgs.at[me], in_sem.at[3])
    own.start()

    load_k.wait()
    rows = pl.ds(pl.multiple_of(r * 8, 8), 8)
    cols = pl.ds(pl.multiple_of(div(c, 2) * 128, 128), 128)
    upper_half = rem(c, 2) == 1
    keep = jnp.where(upper_half, lane, 127 - lane) >= 64
    ratio = []
    for f in range(3):
        k = kap[f, rows, cols]
        k = jnp.where(keep, k, swap(k))
        g = 1.0 / (1.0 + 4.0 * k + react_s[f, f])
        ratio.append(g)
        g2 = g * g
        g4 = g2 * g2
        g8 = g4 * g4
        g16 = g8 * g8
        g32 = g16 * g16
        below = g * (0.5 * drift_s[0, f] - k)
        above = g * (-0.5 * drift_s[0, f] - k)
        after = g * (0.5 * drift_s[1, f] - k)
        before = g * (-0.5 * drift_s[1, f] - k)
        d, e = [n for n in range(3) if n != f]
        coef[0, f] = jnp.where(sub == 7, 0.0, below)
        coef[1, f] = jnp.where(sub == 0, 0.0, above)
        coef[2, f] = jnp.where(inner == 63, 0.0, after)
        coef[3, f] = jnp.where(inner == 0, 0.0, before)
        coef[4, f] = g * react_s[f, d]
        coef[5, f] = g * react_s[f, e]
        coef[6, f] = jnp.where(sub == 7, below, jnp.where(sub == 0, above, 0.0))
        coef[7, f] = jnp.where(inner == 63, after, jnp.where(inner == 0, before, 0.0))
        coef[8, f] = g
        coef[9, f] = g32
        coef[10, f] = 1.0 / (1.0 - ALPHA * (g32 * g32))

    def power(i, carry):
        carry = list(carry)
        for u in range(UNROLL):
            m = i * UNROLL + u
            for f in range(3):
                w, packed = carry[2 * f:2 * f + 2]
                row_g[0, f, pl.ds(m, 1), :] = w[0:1]
                row_g[1, f, pl.ds(m, 1), :] = w[7:8]
                carry[2 * f:2 * f + 2] = [w * coef[8, f], put_columns(m, w, packed)]
        return tuple(carry)

    start = []
    for f in range(3):
        start += [ratio[f], zero]
    ends = lax.fori_loop(0, 32 // UNROLL, power, tuple(start))
    for f in range(3):
        col_g[f] = ends[2 * f + 1]

    left = place_of(r, rem(c + 7, 8), odd_space)
    right = place_of(r, rem(c + 1, 8), odd_space)
    up_in = r > 0
    dn_in = r < 3
    has_up = jnp.logical_or(up_in, sp > 0)
    has_dn = jnp.logical_or(dn_in, sp < spaces - 1)
    up_tm = jnp.where(up_in, place_of(jnp.maximum(r - 1, 0), c, odd_space), me)
    up_sp = jnp.where(up_in, sp, jnp.maximum(sp - 1, 0))
    dn_tm = jnp.where(dn_in, place_of(jnp.minimum(r + 1, 3), c, odd_space), me)
    dn_sp = jnp.where(dn_in, sp, jnp.minimum(sp + 1, spaces - 1))

    def row_copy(j, way):
        return pltpu.make_async_remote_copy(
            src_ref=row_s.at[j, way], dst_ref=row_r.at[j, way], send_sem=h_send.at[j, way], recv_sem=h_recv.at[j, way],
            device_id=((up_tm, up_sp), (dn_tm, dn_sp))[way], device_id_type=MESH)

    def col_copy(j, way):
        return pltpu.make_async_remote_copy(
            src_ref=col_s.at[j], dst_ref=col_r.at[j, way], send_sem=h_send.at[j, 2 + way],
            recv_sem=h_recv.at[j, 2 + way], device_id=((left, right)[way], sp), device_id_type=MESH)

    def carry_in(ends):
        out = []
        for f in range(3):
            end, other = ends[f], swap(ends[f])
            g32 = coef[9, f]
            final = (jnp.where(high, end, other) + g32 * jnp.where(high, other, end)) * coef[10, f]
            wrap = ALPHA * final
            out.append(jnp.where(high, other + g32 * wrap, wrap))
        return out

    def send_halo(j, came, columns):
        for f in range(3):
            x = came[f]
            ahead = jnp.where(even_lane, jnp.where(high, x[:, 64:65], x[:, 0:1]),
                              jnp.where(first_odd, x[:, 63:64], x[:, 127:128]))
            col_s[j, f] = columns[f] + col_g[f] * ahead
        col_copy(j, 0).start()
        col_copy(j, 1).start()
        for f in range(3):
            row_s[j, 0, f] = row_s[j, 0, f] + row_g[0, f] * came[f][0:1]
            row_s[j, 1, f] = row_s[j, 1, f] + row_g[1, f] * came[f][7:8]

        @pl.when(has_up)
        def _():
            row_copy(j, 0).start()

        @pl.when(has_dn)
        def _():
            row_copy(j, 1).start()

    def await_halo(j):
        @pl.when(has_dn)
        def _():
            row_copy(j, 0).wait_recv()

        @pl.when(has_up)
        def _():
            row_copy(j, 1).wait_recv()

        col_copy(j, 0).wait_recv()
        col_copy(j, 1).wait_recv()

    def pack_border(j, m, f, u, packed):
        row_s[j, 0, f, pl.ds(m, 1), :] = u[0:1]
        row_s[j, 1, f, pl.ds(m, 1), :] = u[7:8]
        return put_columns(m, u, packed)

    def interior(came, src, dst):
        def step(i, carry):
            carry = list(carry)
            for u in range(UNROLL):
                m = i * UNROLL + u
                v = []
                for f in range(3):
                    carry[f] = carry[f] * coef[8, f]
                    v.append(src[m, f] + carry[f])
                    if dst is not src:
                        src[m, f] = v[f]
                for f in range(3):
                    d, e = [n for n in range(3) if n != f]
                    off = (coef[0, f] * pltpu.roll(v[f], 7, 0) + coef[1, f] * pltpu.roll(v[f], 1, 0)
                           + coef[2, f] * pltpu.roll(v[f], 127, 1) + coef[3, f] * pltpu.roll(v[f], 1, 1)
                           + coef[4, f] * v[d] + coef[5, f] * v[e])
                    dst[m, f] = held[m, f] - off
            return tuple(carry)

        lax.fori_loop(0, 32 // UNROLL, step, tuple(came))

    def border_scan(j, dst, halo):
        ring = [jnp.where(even_lane, pltpu.roll(col_r[j, 1, f], 65, 1), pltpu.roll(col_r[j, 0, f], 63, 1))
                for f in range(3)]

        def step(i, carry):
            carry = list(carry)
            for u in range(UNROLL):
                m = i * UNROLL + u
                for f in range(3):
                    before, packed = carry[2 * f:2 * f + 2]
                    rows = jnp.where(sub == 0, row_r[j, 1, f, pl.ds(m, 1), :], row_r[j, 0, f, pl.ds(m, 1), :])
                    cols = pltpu.roll(ring[f], rem(128 - 2 * m, 128), 1)
                    x = dst[m, f] - (coef[6, f] * rows + coef[7, f] * cols)
                    now = x + coef[8, f] * before
                    dst[m, f] = now
                    if halo:
                        packed = pack_border(j + 1, m, f, now, packed)
                    carry[2 * f:2 * f + 2] = [now, packed]
            return tuple(carry)

        ends = lax.fori_loop(0, 32 // UNROLL, step, (zero,) * 6)
        return ends[0::2], ends[1::2]

    own.wait()
    some = pl.ds(0, TM - 1)
    pltpu.make_async_copy(pack.at[some], msgs.at[some], a_recv).wait()

    @pl.when(jnp.logical_not(last))
    def _():
        pltpu.make_async_copy(prev_r, prev_r, p_recv).wait()

    for f in range(3):
        p = unfold(prev_r[f])
        msgs[0, f] = msgs[0, f] - ALPHA * jnp.where(high, 0.0, p)

    def first(i, carry):
        carry = list(carry)
        for u in range(UNROLL // 2):
            h = i * (UNROLL // 2) + u
            for f in range(3):
                before, packed = carry[2 * f:2 * f + 2]
                g = coef[8, f]
                a, b = msgs[h, f], msgs[16 + h, f]
                even = g * jnp.where(high, swap(b), a)
                odd = g * jnp.where(high, b, swap(a))
                held[2 * h, f] = even
                held[2 * h + 1, f] = odd
                now = even + g * before
                ua[2 * h, f] = now
                packed = pack_border(0, 2 * h, f, now, packed)
                now = odd + g * now
                ua[2 * h + 1, f] = now
                packed = pack_border(0, 2 * h + 1, f, now, packed)
                carry[2 * f:2 * f + 2] = [now, packed]
        return tuple(carry)

    ends = lax.fori_loop(0, 32 // UNROLL, first, (zero,) * 6)
    came = carry_in(ends[0::2])
    send_halo(0, came, ends[1::2])

    @pl.when(sp > 0)
    def _():
        for n in range(8):
            pl.semaphore_signal(
                ready, inc=1, device_id=(place_of(3, jnp.int32(n), 1 - odd_space), sp - 1), device_id_type=MESH)

    @pl.when(sp < spaces - 1)
    def _():
        for n in range(8):
            pl.semaphore_signal(
                ready, inc=1, device_id=(place_of(0, jnp.int32(n), 1 - odd_space), sp + 1), device_id_type=MESH)

    def sweep(j, came):
        interior(came, ua, ua)
        await_halo(j)
        ends, columns = border_scan(j, ua, True)
        came = carry_in(ends)
        send_halo(j + 1, came, columns)
        return tuple(came)

    came = lax.fori_loop(0, 4, sweep, tuple(came))

    def fold_even(i, carry):
        for u in range(UNROLL // 2):
            h = i * (UNROLL // 2) + u
            for f in range(3):
                even = ua[2 * h, f]
                m5[h, f] = fold_low(even)
                m5[16 + h, f] = fold_high(even)
        return carry

    def to_messages(i, carry):
        carry = list(carry)
        for u in range(UNROLL // 2):
            h = i * (UNROLL // 2) + u
            for f in range(3):
                w = carry[f] * coef[8, f]
                even = ub[2 * h, f] + w
                w = w * coef[8, f]
                odd = ub[2 * h + 1, f] + w
                carry[f] = w
                fifth = ua[2 * h, f]
                one = jnp.where(high, swap(odd), even)
                two = jnp.where(high, odd, swap(even))
                m6[h, f] = one
                m6[16 + h, f] = two
                one = jnp.where(high, 0.0, fifth) * jnp.where(h == 0, 0.0, 1.0) - one
                two = jnp.where(high, 0.0, swap(fifth)) - two
                edge_s[h, f:f + 1, :] = jnp.where(r == 0, one[0:1], one[7:8])
                edge_s[16 + h, f:f + 1, :] = jnp.where(r == 0, two[0:1], two[7:8])
        return tuple(carry)

    def send_back(src, dst, send_sem, recv_sem, own_sem):
        for p in peers:
            pltpu.make_async_remote_copy(
                src_ref=src.at[p], dst_ref=dst.at[tile], send_sem=send_sem, recv_sem=recv_sem,
                device_id=(p, sp), device_id_type=MESH).start()
        own = pltpu.make_async_copy(src.at[me], dst.at[tile], own_sem)
        own.start()
        return own

    interior(came, ua, ub)
    lax.fori_loop(0, 32 // UNROLL, fold_even, 0)
    own5 = send_back(m5, back5, r5_send, r5_recv, in_sem.at[0])
    await_halo(4)
    ends, _ = border_scan(4, ub, False)
    lax.fori_loop(0, 32 // UNROLL, to_messages, tuple(carry_in(ends)))
    own6 = send_back(m6, back6, r6_send, r6_recv, in_sem.at[1])

    def send_edge(way):
        pl.semaphore_wait(ready, TM)
        for o in range(TM):
            p = rem(me + o, TM)
            pltpu.make_async_remote_copy(
                src_ref=edge_s.at[p], dst_ref=edge_r.at[way, c], send_sem=e_send, recv_sem=e_recv.at[way],
                device_id=(p, sp - 1 + 2 * way), device_id_type=MESH).start()

    @pl.when(edge_up)
    def _():
        send_edge(0)

    @pl.when(edge_dn)
    def _():
        send_edge(1)

    own5.wait()
    pltpu.make_async_copy(m5.at[some], back5.at[some], r5_recv).wait()

    first_step = jnp.where(me == 0, 1.0, 0.0)

    @pl.loop(0, 4)
    def _(rr):
        rows = pl.ds(pl.multiple_of(rr * 8, 8), 8)
        for cp in range(4):
            t = rr * 8 + cp * 2
            for f in range(3):
                o0 = jnp.where(high, swap(unfold(back5[t + 1, f])), unfold(back5[t, f]))
                wn[0, f, rows, cp * 128:cp * 128 + 128] = o0 * (1.0 - first_step)

    pltpu.make_async_copy(pack.at[some], msgs.at[some], a_send).wait()

    @pl.when(last)
    def _():
        pltpu.make_async_copy(prev_s.at[some], prev_s.at[some], p_send).wait()

    @pl.loop(0, 5)
    def _(j):
        @pl.when(has_up)
        def _():
            row_copy(j, 0).wait_send()

        @pl.when(has_dn)
        def _():
            row_copy(j, 1).wait_send()

        col_copy(j, 0).wait_send()
        col_copy(j, 1).wait_send()

    own6.wait()
    pltpu.make_async_copy(m6.at[some], back6.at[some], r6_recv).wait()

    @pl.loop(0, 4)
    def _(rr):
        rows = pl.ds(pl.multiple_of(rr * 8, 8), 8)
        for cp in range(4):
            cols = pl.ds(cp * 128, 128)
            t = rr * 8 + cp * 2
            for f in range(3):
                a6, b6 = back6[t, f], back6[t + 1, f]
                n0 = jnp.where(high, swap(b6), a6)
                n1 = jnp.where(high, b6, swap(a6))
                out_u[0, f, rows, cols] = n0
                out_u[1, f, rows, cols] = n1
                wn[0, f, rows, cols] = wn[0, f, rows, cols] - n0
                wn[1, f, rows, cols] = -n1

    @pl.when(sp < spaces - 1)
    def _():
        pltpu.make_async_copy(edge_r.at[0], edge_r.at[0], e_recv.at[0]).wait()

    @pl.when(sp > 0)
    def _():
        pltpu.make_async_copy(edge_r.at[1], edge_r.at[1], e_recv.at[1]).wait()

    high4 = lax.broadcasted_iota(jnp.int32, (4, 128), 1) >= 64
    for way in range(2):
        for cp in range(4):
            a, b = edge_r[way, 2 * cp], edge_r[way, 2 * cp + 1]
            edge_n[way, 0, :, cp * 128:cp * 128 + 128] = jnp.where(high4, swap(b), a)
            edge_n[way, 1, :, cp * 128:cp * 128 + 128] = jnp.where(high4, b, swap(a))

    tall = lax.broadcasted_iota(jnp.int32, (32, 512), 0)
    for s in range(2):
        w = [wn[s, f] for f in range(3)]
        for f in range(3):
            k = kap[f]
            below = jnp.where(tall == 31, edge_n[0, s, f:f + 1, :], pltpu.roll(w[f], 31, 0))
            above = jnp.where(tall == 0, edge_n[1, s, f:f + 1, :], pltpu.roll(w[f], 1, 0))
            after = pltpu.roll(w[f], 511, 1)
            before = pltpu.roll(w[f], 1, 1)
            d, e = [n for n in range(3) if n != f]
            res = (0.5 * drift_s[0, f] * (below - above) + 0.5 * drift_s[1, f] * (after - before)
                   - k * (below + above + after + before) + (react_s[f, d] * w[d] + react_s[f, e] * w[e]))
            own = bv[s, f] - (1.0 + 4.0 * k + react_s[f, f]) * out_u[s, f]
            if s == 0:
                res = res + first_step * own
            else:
                res = res + (own + out_u[0, f])
            out_res[s, f] = res

    pltpu.make_async_copy(m5.at[some], back5.at[some], r5_send).wait()
    pltpu.make_async_copy(m6.at[some], back6.at[some], r6_send).wait()

    @pl.when(jnp.logical_or(edge_up, edge_dn))
    def _():
        pltpu.make_async_copy(edge_s, edge_s, e_send).wait()


def write_out(u, res, out_u, out_res, sem):
    copies = [pltpu.make_async_copy(u, out_u, sem.at[0]), pltpu.make_async_copy(res, out_res, sem.at[1])]
    for copy in copies:
        copy.start()
    for copy in copies:
        copy.wait()


def shards(previous, right_side, kappa, drift, reaction):
    hbm = pl.BlockSpec(memory_space=pltpu.HBM)
    smem = pl.BlockSpec(memory_space=pltpu.SMEM)
    vmem = pl.BlockSpec(memory_space=pltpu.VMEM)
    shape = jax.ShapeDtypeStruct(right_side.shape, F32)
    dma = pltpu.SemaphoreType.DMA
    held = pltpu.VMEM((TM, 3, 8, 128), F32)
    folded = pltpu.VMEM((TM, 3, 4, 128), F32)
    natural = pltpu.VMEM((2, 3, 32, 512), F32)
    results = pl.pallas_call(
        kernel,
        out_shape=(shape, shape),
        in_specs=[hbm, hbm, hbm, smem, smem],
        out_specs=(vmem, vmem),
        scratch_shapes=[
            natural,
            pltpu.VMEM((3, 32, 512), F32),
            pltpu.VMEM((3, 32, 512), F32),
            held, held, held,
            folded, pltpu.VMEM((3, 4, 128), F32),
            held, held, folded, held, folded, held,
            natural,
            pltpu.VMEM((5, 2, 3, 32, 128), F32),
            pltpu.VMEM((5, 2, 3, 32, 128), F32),
            pltpu.VMEM((5, 3, 8, 128), F32),
            pltpu.VMEM((5, 2, 3, 8, 128), F32),
            pltpu.VMEM((TM, 4, 128), F32),
            pltpu.VMEM((2, 8, 4, 128), F32),
            pltpu.VMEM((2, 2, 4, 512), F32),
            pltpu.VMEM((11, 3, 8, 128), F32),
            pltpu.VMEM((2, 3, 32, 128), F32),
            pltpu.VMEM((3, 8, 128), F32),
            dma((4,)),
            dma, dma, dma, dma,
            dma((5, 4)), dma((5, 4)),
            dma, dma, dma, dma,
            dma, dma((2,)), pltpu.SemaphoreType.REGULAR,
        ],
        compiler_params=pltpu.CompilerParams(
            collective_id=0, has_side_effects=True, vmem_limit_bytes=40 * 1024 * 1024),
    )(*[pltpu.with_memory_space_constraint(x, pltpu.HBM) for x in (right_side, previous, kappa, drift.T, reaction)])
    return pl.pallas_call(
        write_out,
        out_shape=(shape, shape),
        in_specs=[vmem, vmem],
        out_specs=(hbm, hbm),
        scratch_shapes=[dma((2,))],
    )(*[pltpu.with_memory_space_constraint(x, pltpu.VMEM) for x in results])


def solution(mesh):
    in_specs = (
        P("tm", None, "space", None),
        P("tm", None, "space", None),
        P(None, "space", None),
        P(),
        P(),
    )
    out_specs = (P("tm", None, "space", None), P("tm", None, "space", None))
    return jax.shard_map(shards, mesh=mesh, in_specs=in_specs, out_specs=out_specs, check_vma=False)
```
